32 devices in a mesh: groups: 2 (over y), space: 4 (over z), tm: 4 (over x, core).
Axes of the slice: x: 2, y: 2, z: 4, core: 2. Of those that a mesh axis runs over, the one named last changes fastest.
Arguments:
- state: float32 [8, 4, 256, 256], P(('groups', 'tm'), 'space'), parts along dimension 0, may hold values from 0 to 1
- classes: int32 [8, 256, 256], P(('groups', 'space')), parts along dimension 0, may hold values from 0 to 3
- perm_table: float32 [4], replicated, may hold values from 0.2 to 2
- rate_table: float32 [4], replicated, may hold values from 0.02 to 1
Outputs:
- new_state: float32 [8, 4, 256, 256], P(('groups', 'tm'), 'space'), parts along dimension 0
The draws below stay inside these ranges and needn't reach their ends.
There are 2 independent parts, one for each index of `groups`. The reference program is written for one: setup_inputs(seed, part) draws one part's arguments, and reference() takes and returns one part's arrays. A program takes and returns all parts, laid end to end along the dimension named above; an argument that names none is the same for every part. Nothing has to cross between parts.
All inputs are finite; a program needn't handle non-finite values.
Results may differ from the reference program's by a relative error of at most 0.0001.
Values sent between devices are 32-bit elements; how exact they have to be, the bound alone decides.
A program may use at most 64 MiB of HBM per device.

```python
import math
import jax
import jax.numpy as jnp

NY = 256
NZ = 256
ITERS = 3
FINE = 2
CLASSES = 4
NT = 4
NX = 4


def set_ends(values, stream_key, smallest, top_value):
    shape = values.shape
    index_at = [jax.random.randint(jax.random.fold_in(stream_key, axis), (), 0, shape[axis]) for axis in range(len(shape))]
    values = values.at[tuple(index_at)].set(smallest)
    longest = shape.index(max(shape))
    index_at[longest] = (index_at[longest] + 1) % shape[longest]
    return values.at[tuple(index_at)].set(top_value)


def levels(rng, shape, cuts, low, high):
    loudness = 1.0
    for position, shards_of in cuts:
        steps = jax.random.uniform(jax.random.fold_in(jax.random.fold_in(rng, 6), position), (shards_of,), jnp.float32, low / len(cuts), high / len(cuts))
        loudness = loudness * jnp.repeat(jnp.exp(steps), shape[position] // shards_of).reshape((-1,) + (1,) * (len(shape) - 1 - position))
    return loudness


def setup_inputs(seed: int = 0, part: int = 0) -> dict:
    streams_of = jax.random.split(jax.random.key(seed), 5)
    own_keys = jax.random.split(jax.random.fold_in(streams_of[4], part), 5)
    state = jnp.clip(1.0 * jax.random.uniform(own_keys[0], (NT, NX, NY, NZ), jnp.float32) ** levels(own_keys[0], (NT, NX, NY, NZ), ((0, 4), (1, 4)), -0.2, 0.2), 0.0, 1.0)
    classes = set_ends(jax.random.randint(own_keys[1], (NX, NY, NZ), 0, CLASSES), jax.random.fold_in(own_keys[1], 1), 0, CLASSES - 1).astype(jnp.int32)
    perm_table = jnp.clip(jnp.exp(jax.random.uniform(streams_of[2], (CLASSES,), jnp.float32, math.log(0.2), math.log(2.0))), 0.2, 2.0)
    rate_table = jnp.clip(jnp.exp(jax.random.uniform(streams_of[3], (CLASSES,), jnp.float32, math.log(0.02), math.log(1.0))), 0.02, 1.0)
    return dict(state=state, classes=classes, perm_table=perm_table, rate_table=rate_table)


DIFF = 2.0
ADV = 0.25


def restrict(field):
    cx, ny, nz = field.shape
    return field.reshape(cx, ny // 2, 2, nz // 2, 2).mean(axis=(2, 4))


def prolong(coarse):
    return jnp.repeat(jnp.repeat(coarse, 2, axis=1), 2, axis=2)


def vertical(field):
    zero_plane = jnp.zeros(field.shape[:2] + (1,), jnp.float32)
    upper = jnp.concatenate([field[:, :, 1:], zero_plane], axis=2)
    lower = jnp.concatenate([zero_plane, field[:, :, :-1]], axis=2)
    return upper, lower


def operate(field):
    upper, lower = vertical(field)
    beside = jnp.roll(field, -1, 0) + jnp.roll(field, 1, 0)
    beside = beside + jnp.roll(field, -1, 1) + jnp.roll(field, 1, 1)
    beside = beside + upper + lower
    return (1.0 + 6.0 * DIFF) * field - DIFF * beside


def fine_step(field, perm):
    upper, lower = vertical(field)
    rhs = field - ADV * perm * field * (upper - lower)
    solution = field
    residual = rhs - operate(solution)
    direction = residual
    norm_now = jnp.sum(residual * residual)
    for step in range(ITERS):
        image = operate(direction)
        alpha = norm_now / jnp.sum(direction * image)
        solution = solution + alpha * direction
        residual = residual - alpha * image
        norm_next = jnp.sum(residual * residual)
        direction = residual + (norm_next / norm_now) * direction
        norm_now = norm_next
    return solution


def reference(state, classes, perm_table, rate_table):
    perm = perm_table[classes]
    rate = rate_table[classes]
    coarse_ratio = 1.0 / (1.0 + restrict(rate))
    jumps = []
    for slice_index in range(NT):
        field = state[slice_index]
        for step in range(FINE):
            field = fine_step(field, perm)
        jumps.append(field - prolong(coarse_ratio * restrict(state[slice_index])))
    outputs = [state[0]]
    coarse = restrict(state[0])
    for slice_index in range(1, NT):
        jump = jumps[slice_index - 1]
        outputs.append(prolong(coarse_ratio * coarse) + jump)
        coarse = coarse_ratio * coarse + restrict(jump)
    return jnp.stack(outputs, axis=0)
```

```python
import functools

import jax
import jax.numpy as jnp
from jax import lax
from jax.experimental import pallas as pl
from jax.experimental.pallas import tpu as pltpu
from jax.sharding import PartitionSpec as P

ITERS = 3
FINE = 2


DIFF = 2.0
ADV = 0.25

CENTRE = 1.0 + 6.0 * DIFF
SCALE = 0.125
BESIDE = DIFF / SCALE
LOWEST = CENTRE - 6.0 * DIFF
HIGHEST = CENTRE + 6.0 * DIFF
HALO = 8
MOMENTS = 2 * ITERS
F32 = jnp.float32
BF16 = jnp.bfloat16


def pieces(value):
    high = value.astype(BF16)
    rest = value - high.astype(F32)
    middle = rest.astype(BF16)
    low = (rest - middle.astype(F32)).astype(BF16)
    return high, middle, low


def times(value, matrix):
    a, b, c = pieces(value)
    dot = functools.partial(jnp.dot, preferred_element_type=F32)
    return dot(a, matrix) + (dot(b, matrix) + dot(c, matrix))


def times_left(matrix, value):
    a, b, c = pieces(value)
    dot = functools.partial(jnp.dot, preferred_element_type=F32)
    return dot(matrix, a) + (dot(matrix, b) + dot(matrix, c))


def pairs(small, large, along, value):
    i = lax.broadcasted_iota(jnp.int32, (small, large) if along else (large, small), 0 if along else 1)
    j = lax.broadcasted_iota(jnp.int32, (small, large) if along else (large, small), 1 if along else 0)
    off = j - 2 * i
    return jnp.where((off == 0) | (off == 1), value, 0.0).astype(BF16)


def restricted(field):
    ny, nz = field.shape
    narrow = times(field, pairs(nz // 2, nz, False, 0.5))
    return times_left(pairs(ny // 2, ny, True, 0.5), narrow)


def prolonged(coarse):
    cy, cz = coarse.shape
    right = pairs(cz, 2 * cz, True, 1.0)
    left = pairs(cy, 2 * cy, False, 1.0)
    dot = functools.partial(jnp.dot, preferred_element_type=F32)
    total = None
    for piece in pieces(coarse):
        wide = dot(left, dot(piece, right).astype(BF16))
        total = wide if total is None else total + wide
    return total


def looked_up(table_ref, classes):
    values = jnp.full(classes.shape, table_ref[0], F32)
    for entry in range(1, table_ref.shape[0]):
        values = jnp.where(classes == entry, table_ref[entry], values)
    return values


def coefficients(moments):
    def inner(a, b):
        total = None
        for i, x in enumerate(a):
            for j, y in enumerate(b):
                term = x * y * moments[i + j]
                total = term if total is None else total + term
        return total

    one = jnp.ones_like(moments[0])
    residual, direction, solution = [one], [one], []
    norm_now = moments[0]
    for step in range(ITERS):
        image = [CENTRE * d for d in direction] + [0.0 * one]
        for i, d in enumerate(direction):
            image[i + 1] = image[i + 1] - BESIDE * d
        alpha = norm_now / inner(direction, image)
        alpha = jnp.clip(alpha, 1.0 / HIGHEST, 1.0 / LOWEST)
        for i, d in enumerate(direction):
            if i < len(solution):
                solution[i] = solution[i] + alpha * d
            else:
                solution.append(alpha * d)
        if step == ITERS - 1:
            break
        residual = residual + [0.0 * one]
        residual = [r - alpha * a for r, a in zip(residual, image)]
        norm_next = inner(residual, residual)
        beta = jnp.clip(norm_next / norm_now, 0.0, HIGHEST - LOWEST)
        direction = [r + beta * d for r, d in zip(residual, direction + [0.0 * one])]
        norm_now = norm_next
    return solution


def kernel(S, T, state_ref, classes_ref, perm_ref, rate_ref, out_ref,
           ext, extk, cbuf, kbuf, nbuf, dbuf, w0, w1, w2, w3, d0, d1, d2, perm_buf,
           q_buf, msrc, mbuf, jsrc, jbuf, gsrc, gbuf, ssrc, sbuf,
           local_sem, c_send, c_recv, k_send, k_recv, m_send, m_recv,
           j_send, j_recv, g_send, g_recv, s_send, s_recv):
    NY, NZ = state_ref.shape
    rows = NY // S
    slab = rows + 2 * HALO
    own = slice(HALO, HALO + rows)
    me = lax.axis_index("space")
    t = lax.axis_index("tm")

    local = []
    for n, (source, target) in enumerate(((state_ref, ext), (classes_ref, extk))):
        local += [
            pltpu.make_async_copy(source, target.at[pl.ds(HALO, NY)], local_sem.at[3 * n]),
            pltpu.make_async_copy(
                source.at[pl.ds(NY - HALO, HALO)], target.at[pl.ds(0, HALO)], local_sem.at[3 * n + 1]),
            pltpu.make_async_copy(
                source.at[pl.ds(0, HALO)], target.at[pl.ds(HALO + NY, HALO)], local_sem.at[3 * n + 2]),
        ]
    for copy in local:
        copy.start()

    barrier = pltpu.get_barrier_semaphore()
    for dt in range(T):
        for dz in range(S):
            if dt or dz:
                pl.semaphore_signal(
                    barrier, inc=1,
                    device_id={"tm": lax.rem(t + dt, T), "space": lax.rem(me + dz, S)},
                    device_id_type=pl.DeviceIdType.MESH)
    for copy in local:
        copy.wait()
    pl.semaphore_wait(barrier, S * T - 1)

    def slab_copy(source, target, send, recv, d):
        to = lax.rem(me + d, S)
        return pltpu.make_async_remote_copy(
            src_ref=source.at[pl.ds(pl.multiple_of(to * rows, 8), slab)],
            dst_ref=target.at[me],
            send_sem=send.at[d - 1], recv_sem=recv.at[d - 1],
            device_id={"space": to}, device_id_type=pl.DeviceIdType.MESH)

    c_copies = [slab_copy(ext, cbuf, c_send, c_recv, d) for d in range(1, S)]
    k_copies = [slab_copy(extk, kbuf, k_send, k_recv, d) for d in range(1, S)]
    for copy in c_copies:
        copy.start()
    for copy in k_copies:
        copy.start()
    mine = pl.ds(pl.multiple_of(me * rows, 8), slab)
    cbuf[me] = ext[mine]
    kbuf[me] = extk[mine]

    ssrc[...] = restricted(ext[HALO:HALO + NY])
    s_copies = [
        pltpu.make_async_remote_copy(
            src_ref=ssrc, dst_ref=sbuf, send_sem=s_send.at[d - 1], recv_sem=s_recv.at[0],
            device_id={"tm": lax.rem(t + d, T)}, device_id_type=pl.DeviceIdType.MESH)
        for d in range(1, T)
    ]

    @pl.when(t == 0)
    def _():
        for copy in s_copies:
            copy.start()

    out_ratio = 1.0 / (1.0 + restricted(looked_up(rate_ref, extk[HALO:HALO + NY])))

    i = lax.broadcasted_iota(jnp.int32, (NZ, NZ), 0)
    j = lax.broadcasted_iota(jnp.int32, (NZ, NZ), 1)
    up, down = i - j == 1, j - i == 1
    both = jnp.where(up | down, 1.0, 0.0).astype(BF16)
    apart = jnp.where(up, 1.0, jnp.where(down, -1.0, 0.0)).astype(BF16)

    def neighbours(ref, p):
        value = ref[p]
        total = times(value, both)
        total = total + (ref[(p + 1) % S] + ref[(p + S - 1) % S])
        total = total + (pltpu.roll(value, 1, 0) + pltpu.roll(value, slab - 1, 0))
        return SCALE * total

    def dot_rows(a, b):
        product = (a * b)[own]
        return product.reshape(rows // 8, 8, NZ).sum(axis=0)

    for copy in c_copies:
        copy.wait_recv()
    for p in range(S):
        nbuf[p] = neighbours(cbuf, p)
        dbuf[p] = times(cbuf[p], apart)
    for copy in k_copies:
        copy.wait_recv()
    for p in range(S):
        c = cbuf[p]
        perm = looked_up(perm_ref, kbuf[p])
        perm_buf[p] = perm
        w0[p] = c - ADV * perm * c * dbuf[p] - CENTRE * c + BESIDE * nbuf[p]

    krylov = (w0, w1, w2, w3)
    for fine in range(FINE):
        sums = [None] * MOMENTS
        for k in range(ITERS):
            source, target = krylov[k], krylov[k + 1]
            for p in range(S):
                value = neighbours(source, p)
                target[p] = value
                here = source[p]
                for order, term in ((2 * k, dot_rows(here, here)), (2 * k + 1, dot_rows(here, value))):
                    sums[order] = term if sums[order] is None else sums[order] + term
        lines = [jnp.sum(s[:, :NZ // 2] + s[:, NZ // 2:], axis=0, keepdims=True) for s in sums]
        lines = lines + [jnp.zeros_like(lines[0])] * (8 - MOMENTS)
        msrc[fine] = jnp.concatenate(lines, axis=0)
        mbuf[fine, me] = msrc[fine]
        m_copies = [
            pltpu.make_async_remote_copy(
                src_ref=msrc.at[fine], dst_ref=mbuf.at[fine, me],
                send_sem=m_send.at[fine, d - 1], recv_sem=m_recv.at[fine, d - 1],
                device_id={"space": lax.rem(me + d, S)}, device_id_type=pl.DeviceIdType.MESH)
            for d in range(1, S)
        ]
        for copy in m_copies:
            copy.start()
        if fine < FINE - 1:
            for p in range(S):
                d0[p] = times(w0[p], apart)
                d1[p] = times(w1[p], apart)
                d2[p] = times(w2[p], apart)
        if fine == 0:
            whole = jnp.concatenate([cbuf[p][own] for p in range(S)], axis=0)
            kinds = jnp.concatenate([kbuf[p][own] for p in range(S)], axis=0)
            ratio = 1.0 / (1.0 + restricted(looked_up(rate_ref, kinds)))
            q_buf[...] = ratio * restricted(whole)
        if fine == FINE - 1:
            from_start = prolonged(q_buf[...])
            for p in range(S):
                jsrc[p] = cbuf[p][own] - from_start[p * rows:(p + 1) * rows]
        for copy in m_copies:
            copy.wait()
        total = mbuf[fine, 0]
        for d in range(1, S):
            total = total + mbuf[fine, d]
        total = jnp.sum(total, axis=1, keepdims=True)
        found = [jnp.broadcast_to(total[k:k + 1, :], (1, NZ)) for k in range(MOMENTS)]
        a = coefficients(found)
        if fine < FINE - 1:
            for p in range(S):
                x0, x1, x2, x3 = w0[p], w1[p], w2[p], w3[p]
                c = cbuf[p] + a[0] * x0 + a[1] * x1 + a[2] * x2
                near = nbuf[p] + a[0] * x1 + a[1] * x2 + a[2] * x3
                apart_c = dbuf[p] + a[0] * d0[p] + a[1] * d1[p] + a[2] * d2[p]
                cbuf[p] = c
                nbuf[p] = near
                dbuf[p] = apart_c
                w0[p] = c - ADV * perm_buf[p] * c * apart_c - CENTRE * c + BESIDE * near
        else:
            for p in range(S):
                jsrc[p] += a[0] * w0[p][own] + a[1] * w1[p][own] + a[2] * w2[p][own]

    def jump_copy(p):
        return pltpu.make_async_remote_copy(
            src_ref=jsrc.at[p], dst_ref=jbuf.at[me],
            send_sem=j_send.at[p], recv_sem=j_recv.at[me],
            device_id={"tm": lax.rem(t + 1, T), "space": p}, device_id_type=pl.DeviceIdType.MESH)

    def coarse_copy(p, ahead):
        return pltpu.make_async_remote_copy(
            src_ref=gsrc.at[p], dst_ref=gbuf.at[lax.rem(t, T - 2), me],
            send_sem=g_send.at[ahead - 2, p], recv_sem=g_recv.at[lax.rem(t, T - 2), me],
            device_id={"tm": lax.rem(t + ahead, T), "space": p}, device_id_type=pl.DeviceIdType.MESH)

    @pl.when(t < T - 1)
    def _():
        for p in range(S):
            jump_copy(p).start()

    @pl.when(t < T - 2)
    def _():
        jump = jsrc[...].reshape(NY, NZ)
        gsrc[...] = restricted(jump).reshape(S, rows // 2, NZ // 2)
        for ahead in range(2, T):
            @pl.when(t + ahead < T)
            def _():
                for p in range(S):
                    coarse_copy(p, ahead).start()

    @pl.when(t == 0)
    def _():
        out_ref[...] = ext[HALO:HALO + NY]
        for copy in s_copies:
            copy.wait_send()

    @pl.when(t > 0)
    def _():
        s_copies[0].wait_recv()
        for k in range(T - 2):
            @pl.when(k < t - 1)
            def _():
                for p in range(S):
                    pltpu.make_async_remote_copy(
                        src_ref=gsrc.at[p], dst_ref=gbuf.at[k, p],
                        send_sem=g_send.at[0, p], recv_sem=g_recv.at[k, p],
                        device_id={"tm": lax.rem(t + 1, T), "space": p},
                        device_id_type=pl.DeviceIdType.MESH).wait_recv()
                sbuf[...] = out_ratio * sbuf[...] + gbuf[k].reshape(NY // 2, NZ // 2)
        wide = prolonged(out_ratio * sbuf[...])
        for p in range(S):
            pltpu.make_async_remote_copy(
                src_ref=jsrc.at[p], dst_ref=jbuf.at[p],
                send_sem=j_send.at[p], recv_sem=j_recv.at[p],
                device_id={"tm": lax.rem(t + 1, T), "space": p},
                device_id_type=pl.DeviceIdType.MESH).wait_recv()
        out_ref[...] = wide + jbuf[...].reshape(NY, NZ)

    for copy in c_copies:
        copy.wait_send()
    for copy in k_copies:
        copy.wait_send()

    @pl.when(t < T - 1)
    def _():
        for p in range(S):
            jump_copy(p).wait_send()
    for ahead in range(2, T):
        @pl.when(t + ahead < T)
        def _():
            for p in range(S):
                coarse_copy(p, ahead).wait_send()


def fused_body(S, T, state, classes, perm_table, rate_table):
    ny, nz = state.shape[2:]
    rows = ny // S
    slab = rows + 2 * HALO
    field = pltpu.VMEM((S, slab, nz), F32)
    dma = pltpu.SemaphoreType.DMA
    updated = pl.pallas_call(
        functools.partial(kernel, S, T),
        out_shape=jax.ShapeDtypeStruct((ny, nz), F32),
        in_specs=[
            pl.BlockSpec(memory_space=pl.ANY),
            pl.BlockSpec(memory_space=pl.ANY),
            pl.BlockSpec(memory_space=pltpu.SMEM),
            pl.BlockSpec(memory_space=pltpu.SMEM),
        ],
        out_specs=pl.BlockSpec(memory_space=pltpu.VMEM),
        scratch_shapes=[
            pltpu.VMEM((ny + 2 * HALO, nz), F32),
            pltpu.VMEM((ny + 2 * HALO, nz), jnp.int32),
            field,
            pltpu.VMEM((S, slab, nz), jnp.int32),
        ] + [field] * 10 + [
            pltpu.VMEM((ny // 2, nz // 2), F32),
            pltpu.VMEM((FINE, 8, nz // 2), F32),
            pltpu.VMEM((FINE, S, 8, nz // 2), F32),
            pltpu.VMEM((S, rows, nz), F32),
            pltpu.VMEM((S, rows, nz), F32),
            pltpu.VMEM((S, rows // 2, nz // 2), F32),
            pltpu.VMEM((T - 2, S, rows // 2, nz // 2), F32),
            pltpu.VMEM((ny // 2, nz // 2), F32),
            pltpu.VMEM((ny // 2, nz // 2), F32),
            dma((6,)),
            dma((S - 1,)), dma((S - 1,)),
            dma((S - 1,)), dma((S - 1,)),
            dma((FINE, S - 1)), dma((FINE, S - 1)),
            dma((S,)), dma((S,)),
            dma((T - 2, S)), dma((T - 2, S)),
            dma((T - 1,)), dma((1,)),
        ],
        compiler_params=pltpu.CompilerParams(
            collective_id=0, has_side_effects=True, vmem_limit_bytes=40 * 1024 * 1024),
    )(state[0, 0], classes[0], perm_table, rate_table)
    return updated[None, None]


def with_halo(array, sides, width):
    for axis, dim in sides:
        devices, length = (lax.axis_size(axis), array.shape[dim])
        up = [(i, (i + 1) % devices) for i in range(devices)]
        down = [(j, i) for i, j in up]
        last = lax.slice_in_dim(array, length - width, length, axis=dim)
        first = lax.slice_in_dim(array, 0, width, axis=dim)
        before = lax.ppermute(last, axis, up)
        after = lax.ppermute(first, axis, down)
        array = jnp.concatenate([before, array, after], axis=dim)
    return array


def passed_along(array, axis, by):
    devices = lax.axis_size(axis)
    pairs = [(i, i + by) for i in range(devices) if 0 <= i + by < devices]
    return lax.ppermute(array, axis, pairs)


def lookup(table, classes):
    values = jnp.zeros(classes.shape, jnp.float32)
    for entry in range(table.shape[0]):
        values = jnp.where(classes == entry, table[entry], values)
    return values


def restrict(field):
    cx, ny, nz = field.shape
    return field.reshape(cx, ny // 2, 2, nz // 2, 2).mean(axis=(2, 4))


def prolong(coarse):
    return jnp.repeat(jnp.repeat(coarse, 2, axis=1), 2, axis=2)


def vertical(field):
    zero_plane = jnp.zeros(field.shape[:2] + (1,), jnp.float32)
    upper = jnp.concatenate([field[:, :, 1:], zero_plane], axis=2)
    lower = jnp.concatenate([zero_plane, field[:, :, :-1]], axis=2)
    return (upper, lower)


def operate(field):
    padded = with_halo(field, (("space", 0),), 1)
    upper, lower = vertical(field)
    beside = padded[2:] + padded[:-2]
    beside = beside + jnp.roll(field, -1, 1) + jnp.roll(field, 1, 1)
    beside = beside + upper + lower
    return (1.0 + 6.0 * DIFF) * field - DIFF * beside


def squares(residual):
    return lax.psum(jnp.sum(residual * residual), "space")


def fine_step(field, perm):
    upper, lower = vertical(field)
    rhs = field - ADV * perm * field * (upper - lower)
    solution = field
    residual = rhs - operate(solution)
    direction = residual
    norm_now = squares(residual)
    for step in range(ITERS):
        image = operate(direction)
        alpha = norm_now / lax.psum(jnp.sum(direction * image), "space")
        solution = solution + alpha * direction
        residual = residual - alpha * image
        norm_next = squares(residual)
        direction = residual + norm_next / norm_now * direction
        norm_now = norm_next
    return solution


def body(state, classes, perm_table, rate_table):
    start = state[0]
    perm = lookup(perm_table, classes)
    coarse_ratio = 1.0 / (1.0 + restrict(lookup(rate_table, classes)))
    field = start
    for step in range(FINE):
        field = fine_step(field, perm)
    coarse_start = restrict(start)
    jump = field - prolong(coarse_ratio * coarse_start)
    jump_coarse = restrict(jump)
    first = lax.axis_index("tm") == 0
    factor = jnp.where(first, 0.0, coarse_ratio)
    offset = jnp.where(first, coarse_ratio * coarse_start + jump_coarse, jump_coarse)
    before = passed_along(jump, "tm", 1)
    before_coarse = restrict(before)

    def relay_turn(turn, carry):
        outgoing, received = carry
        received = passed_along(outgoing, "tm", 1)
        return (factor * received + offset, received)

    outgoing, received = lax.fori_loop(
        0, lax.axis_size("tm") - 1, relay_turn, (offset, jnp.zeros_like(offset))
    )
    updated = jnp.where(first, start, before + prolong(received - before_coarse))
    return updated[None]


def solution(mesh):
    placed = (
        P(("groups", "tm"), "space", None, None),
        P(("groups", "space"), None, None),
        P(),
        P(),
    )
    devices, slices = (mesh.shape["space"], mesh.shape["tm"])

    def chosen(state, classes, perm_table, rate_table):
        planes, ny, nz = state.shape[1:]
        fits = planes == 1 and ny // devices >= 4 * HALO and nz % 256 == 0
        if fits and slices >= 3 and devices >= 3:
            return fused_body(devices, slices, state, classes, perm_table, rate_table)
        return body(state, classes, perm_table, rate_table)

    return jax.shard_map(
        chosen,
        mesh=mesh,
        in_specs=placed,
        out_specs=P(("groups", "tm"), "space", None, None),
        check_vma=False,
    )
```

```python
import functools

import jax
import jax.numpy as jnp
from jax import lax
from jax.experimental import pallas as pl
from jax.experimental.pallas import tpu as pltpu
from jax.sharding import PartitionSpec as P

ITERS = 3
FINE = 2


DIFF = 2.0
ADV = 0.25

CENTRE = 1.0 + 6.0 * DIFF
SCALE = 0.125
BESIDE = DIFF / SCALE
LOWEST = CENTRE - 6.0 * DIFF
HIGHEST = CENTRE + 6.0 * DIFF
HALO = 8
MOMENTS = 2 * ITERS
F32 = jnp.float32
BF16 = jnp.bfloat16


def pieces(value):
    high = value.astype(BF16)
    rest = value - high.astype(F32)
    middle = rest.astype(BF16)
    low = (rest - middle.astype(F32)).astype(BF16)
    return high, middle, low


def times(value, matrix):
    a, b, c = pieces(value)
    dot = functools.partial(jnp.dot, preferred_element_type=F32)
    return dot(a, matrix) + (dot(b, matrix) + dot(c, matrix))


def times_left(matrix, value):
    a, b, c = pieces(value)
    dot = functools.partial(jnp.dot, preferred_element_type=F32)
    return dot(matrix, a) + (dot(matrix, b) + dot(matrix, c))


def pairs(small, large, along, value):
    i = lax.broadcasted_iota(jnp.int32, (small, large) if along else (large, small), 0 if along else 1)
    j = lax.broadcasted_iota(jnp.int32, (small, large) if along else (large, small), 1 if along else 0)
    off = j - 2 * i
    return jnp.where((off == 0) | (off == 1), value, 0.0).astype(BF16)


def restricted(field):
    ny, nz = field.shape
    narrow = times(field, pairs(nz // 2, nz, False, 0.5))
    return times_left(pairs(ny // 2, ny, True, 0.5), narrow)


def prolonged(coarse):
    cy, cz = coarse.shape
    right = pairs(cz, 2 * cz, True, 1.0)
    left = pairs(cy, 2 * cy, False, 1.0)
    dot = functools.partial(jnp.dot, preferred_element_type=F32)
    total = None
    for piece in pieces(coarse):
        wide = dot(left, dot(piece, right).astype(BF16))
        total = wide if total is None else total + wide
    return total


def looked_up(table_ref, classes):
    values = jnp.full(classes.shape, table_ref[0], F32)
    for entry in range(1, table_ref.shape[0]):
        values = jnp.where(classes == entry, table_ref[entry], values)
    return values


def coefficients(moments):
    def inner(a, b):
        total = None
        for i, x in enumerate(a):
            for j, y in enumerate(b):
                term = x * y * moments[i + j]
                total = term if total is None else total + term
        return total

    one = jnp.ones_like(moments[0])
    residual, direction, solution = [one], [one], []
    norm_now = moments[0]
    for step in range(ITERS):
        image = [CENTRE * d for d in direction] + [0.0 * one]
        for i, d in enumerate(direction):
            image[i + 1] = image[i + 1] - BESIDE * d
        alpha = norm_now / inner(direction, image)
        alpha = jnp.clip(alpha, 1.0 / HIGHEST, 1.0 / LOWEST)
        for i, d in enumerate(direction):
            if i < len(solution):
                solution[i] = solution[i] + alpha * d
            else:
                solution.append(alpha * d)
        if step == ITERS - 1:
            break
        residual = residual + [0.0 * one]
        residual = [r - alpha * a for r, a in zip(residual, image)]
        norm_next = inner(residual, residual)
        beta = jnp.clip(norm_next / norm_now, 0.0, HIGHEST - LOWEST)
        direction = [r + beta * d for r, d in zip(residual, direction + [0.0 * one])]
        norm_now = norm_next
    return solution


def kernel(S, T, state_ref, classes_ref, perm_hbm, rate_hbm, out_ref,
           ext, extk, cbuf, kbuf, nbuf, dbuf, w0, w1, w2, w3, d0, d1, d2, perm_buf,
           perm_ref, rate_ref, rs_buf, ratio_buf, msrc, mbuf, jsrc, jbuf, gsrc, gbuf, hsrc, hbuf,
           local_sem, c_send, c_recv, k_send, k_recv, f_send, f_recv, m_send, m_recv,
           j_send, j_recv, g_send, g_recv, h_send, h_recv):
    NY, NZ = state_ref.shape
    rows = NY // S
    slab = rows + 2 * HALO
    own = slice(HALO, HALO + rows)
    me = lax.axis_index("space")
    t = lax.axis_index("tm")

    local = []
    for n, (source, target) in enumerate(((state_ref, ext), (classes_ref, extk))):
        local += [
            pltpu.make_async_copy(source, target.at[pl.ds(HALO, NY)], local_sem.at[3 * n]),
            pltpu.make_async_copy(
                source.at[pl.ds(NY - HALO, HALO)], target.at[pl.ds(0, HALO)], local_sem.at[3 * n + 1]),
            pltpu.make_async_copy(
                source.at[pl.ds(0, HALO)], target.at[pl.ds(HALO + NY, HALO)], local_sem.at[3 * n + 2]),
        ]
    local += [
        pltpu.make_async_copy(perm_hbm, perm_ref, local_sem.at[6]),
        pltpu.make_async_copy(rate_hbm, rate_ref, local_sem.at[7]),
    ]
    for copy in local:
        copy.start()

    barrier = pltpu.get_barrier_semaphore()
    partners = [(dt, dz) for dt in range(T) for dz in range(S) if dz == 0 or dt in (0, 1, T - 1)][1:]
    for dt, dz in partners:
        pl.semaphore_signal(
            barrier, inc=1,
            device_id={"tm": lax.rem(t + dt, T), "space": lax.rem(me + dz, S)},
            device_id_type=pl.DeviceIdType.MESH)
    for copy in local:
        copy.wait()
    pl.semaphore_wait(barrier, len(partners))

    high, wide = slab // 2, NZ // 2
    row_part, lane_part = lax.rem(t, 2), lax.div(t, 2)
    lanes = pl.ds(pl.multiple_of(lane_part * wide, 128), wide)
    quarter_rows = pl.ds(pl.multiple_of(row_part * high, 8), high)

    def class_copy(d):
        to = lax.rem(me + d, S)
        start = pl.multiple_of(to * rows + row_part * high, 8)
        return pltpu.make_async_remote_copy(
            src_ref=extk.at[pl.ds(start, high), lanes],
            dst_ref=kbuf.at[me, quarter_rows, lanes],
            send_sem=k_send.at[d - 1], recv_sem=k_recv.at[d - 1],
            device_id={"space": to}, device_id_type=pl.DeviceIdType.MESH)

    def class_forward(d, e):
        place = kbuf.at[lax.rem(me + S - d, S), quarter_rows, lanes]
        return pltpu.make_async_remote_copy(
            src_ref=place, dst_ref=place,
            send_sem=f_send.at[d - 1, e - 1], recv_sem=f_recv.at[d - 1, e - 1],
            device_id={"tm": lax.rem(t + e, T)}, device_id_type=pl.DeviceIdType.MESH)

    def slab_copy(d):
        to = lax.rem(me + d, S)
        return pltpu.make_async_remote_copy(
            src_ref=ext.at[pl.ds(pl.multiple_of(to * rows, 8), slab)],
            dst_ref=cbuf.at[me],
            send_sem=c_send.at[d - 1], recv_sem=c_recv.at[d - 1],
            device_id={"space": to}, device_id_type=pl.DeviceIdType.MESH)

    k_copies = [class_copy(d) for d in range(1, S)]
    c_copies = [slab_copy(d) for d in range(1, S)]
    f_copies = [class_forward(d, e) for d in range(1, S) for e in range(1, T)]
    for copy in k_copies:
        copy.start()
    for copy in c_copies:
        copy.start()
    mine = pl.ds(pl.multiple_of(me * rows, 8), slab)
    cbuf[me] = ext[mine]
    kbuf[me] = extk[mine]

    @pl.when(t == 0)
    def _():
        out_ref[...] = ext[HALO:HALO + NY]

    for d in range(1, S):
        k_copies[d - 1].wait_recv()
        for e in range(1, T):
            f_copies[(d - 1) * (T - 1) + e - 1].start()

    i = lax.broadcasted_iota(jnp.int32, (NZ, NZ), 0)
    j = lax.broadcasted_iota(jnp.int32, (NZ, NZ), 1)
    up, down = i - j == 1, j - i == 1
    both = jnp.where(up | down, 1.0, 0.0).astype(BF16)
    apart = jnp.where(up, 1.0, jnp.where(down, -1.0, 0.0)).astype(BF16)

    def neighbours(ref, p):
        value = ref[p]
        total = times(value, both)
        total = total + (ref[(p + 1) % S] + ref[(p + S - 1) % S])
        total = total + (pltpu.roll(value, 1, 0) + pltpu.roll(value, slab - 1, 0))
        return SCALE * total

    def dot_rows(a, b):
        product = (a * b)[own]
        return product.reshape(rows // 8, 8, NZ).sum(axis=0)

    for copy in c_copies:
        copy.wait_recv()
    for p in range(S):
        nbuf[p] = neighbours(cbuf, p)
        dbuf[p] = times(cbuf[p], apart)
    for copy in f_copies:
        copy.wait_recv()
    for p in range(S):
        c = cbuf[p]
        perm = looked_up(perm_ref, kbuf[p])
        perm_buf[p] = perm
        w0[p] = c - ADV * perm * c * dbuf[p] - CENTRE * c + BESIDE * nbuf[p]

    def arriving(source, target, send, recv, p):
        return pltpu.make_async_remote_copy(
            src_ref=source, dst_ref=target, send_sem=send, recv_sem=recv,
            device_id={"tm": lax.rem(t + 1, T), "space": p}, device_id_type=pl.DeviceIdType.MESH)

    def jump_copy(p):
        return arriving(jsrc.at[p], jbuf.at[me], j_send.at[p], j_recv.at[me], p)

    def coarse_copy(p):
        return arriving(gsrc.at[p], gbuf.at[me], g_send.at[p], g_recv.at[me], p)

    chain_copy = arriving(hsrc, hbuf, h_send.at[0], h_recv.at[0], me)

    krylov = (w0, w1, w2, w3)
    for fine in range(FINE):
        sums = [None] * MOMENTS
        for k in range(ITERS):
            source, target = krylov[k], krylov[k + 1]
            for p in range(S):
                value = neighbours(source, p)
                target[p] = value
                here = source[p]
                for order, term in ((2 * k, dot_rows(here, here)), (2 * k + 1, dot_rows(here, value))):
                    sums[order] = term if sums[order] is None else sums[order] + term
        lines = [jnp.sum(s[:, :NZ // 2] + s[:, NZ // 2:], axis=0, keepdims=True) for s in sums]
        lines = lines + [jnp.zeros_like(lines[0])] * (8 - MOMENTS)
        msrc[fine] = jnp.concatenate(lines, axis=0)
        mbuf[fine, me] = msrc[fine]
        m_copies = [
            pltpu.make_async_remote_copy(
                src_ref=msrc.at[fine], dst_ref=mbuf.at[fine, me],
                send_sem=m_send.at[fine, d - 1], recv_sem=m_recv.at[fine, d - 1],
                device_id={"space": lax.rem(me + d, S)}, device_id_type=pl.DeviceIdType.MESH)
            for d in range(1, S)
        ]
        for copy in m_copies:
            copy.start()
        if fine < FINE - 1:
            for p in range(S):
                d0[p] = times(w0[p], apart)
                d1[p] = times(w1[p], apart)
                d2[p] = times(w2[p], apart)
        if fine == 0:
            whole = jnp.concatenate([cbuf[p][own] for p in range(S)], axis=0)
            kinds = jnp.concatenate([kbuf[p][own] for p in range(S)], axis=0)
            ratio_buf[...] = 1.0 / (1.0 + restricted(looked_up(rate_ref, kinds)))
            rs_buf[...] = restricted(whole)
        for copy in m_copies:
            copy.wait()
        total = mbuf[fine, 0]
        for d in range(1, S):
            total = total + mbuf[fine, d]
        total = jnp.sum(total, axis=1, keepdims=True)
        found = [jnp.broadcast_to(total[k:k + 1, :], (1, NZ)) for k in range(MOMENTS)]
        a = coefficients(found)
        if fine < FINE - 1:
            for p in range(S):
                x0, x1, x2, x3 = w0[p], w1[p], w2[p], w3[p]
                c = cbuf[p] + a[0] * x0 + a[1] * x1 + a[2] * x2
                near = nbuf[p] + a[0] * x1 + a[1] * x2 + a[2] * x3
                apart_c = dbuf[p] + a[0] * d0[p] + a[1] * d1[p] + a[2] * d2[p]
                cbuf[p] = c
                nbuf[p] = near
                dbuf[p] = apart_c
                w0[p] = c - ADV * perm_buf[p] * c * apart_c - CENTRE * c + BESIDE * near
        else:
            for p in range(S):
                jsrc[p] = cbuf[p][own] + (a[0] * w0[p][own] + a[1] * w1[p][own] + a[2] * w2[p][own])

                @pl.when(t < T - 1)
                def _():
                    jump_copy(p).start()

    @pl.when(t < T - 2)
    def _():
        hsrc[...] = restricted(jsrc[...].reshape(NY, NZ))

    @pl.when((t > 0) & (t < T - 1))
    def _():
        chain_copy.wait_recv()
        correction = ratio_buf[...] * (hbuf[...] - rs_buf[...])
        gsrc[...] = correction.reshape(S, rows // 2, NZ // 2)

    @pl.when((t > 0) & (t < T - 2))
    def _():
        hsrc[...] += gsrc[...].reshape(NY // 2, NZ // 2)

    @pl.when(t < T - 2)
    def _():
        chain_copy.start()

    @pl.when((t > 0) & (t < T - 1))
    def _():
        for p in range(S):
            coarse_copy(p).start()

    @pl.when(t > 1)
    def _():
        for p in range(S):
            arriving(gsrc.at[p], gbuf.at[p], g_send.at[p], g_recv.at[p], p).wait_recv()
        out_ref[...] = prolonged(gbuf[...].reshape(NY // 2, NZ // 2))

    @pl.when(t == 1)
    def _():
        out_ref[...] = jnp.zeros_like(out_ref)

    @pl.when(t > 0)
    def _():
        for p in range(S):
            arriving(jsrc.at[p], jbuf.at[p], j_send.at[p], j_recv.at[p], p).wait_recv()
        out_ref[...] += jbuf[...].reshape(NY, NZ)

    for copy in c_copies + k_copies + f_copies:
        copy.wait_send()

    @pl.when(t < T - 1)
    def _():
        for p in range(S):
            jump_copy(p).wait_send()

    @pl.when(t < T - 2)
    def _():
        chain_copy.wait_send()

    @pl.when((t > 0) & (t < T - 1))
    def _():
        for p in range(S):
            coarse_copy(p).wait_send()


def fused_body(S, T, state, classes, perm_table, rate_table):
    ny, nz = state.shape[2:]
    rows = ny // S
    slab = rows + 2 * HALO
    field = pltpu.VMEM((S, slab, nz), F32)
    coarse = pltpu.VMEM((ny // 2, nz // 2), F32)
    dma = pltpu.SemaphoreType.DMA
    updated = pl.pallas_call(
        functools.partial(kernel, S, T),
        out_shape=jax.ShapeDtypeStruct((ny, nz), F32),
        in_specs=[pl.BlockSpec(memory_space=pltpu.HBM)] * 4,
        out_specs=pl.BlockSpec(memory_space=pltpu.VMEM),
        scratch_shapes=[
            pltpu.VMEM((ny + 2 * HALO, nz), F32),
            pltpu.VMEM((ny + 2 * HALO, nz), jnp.int32),
            field,
            pltpu.VMEM((S, slab, nz), jnp.int32),
        ] + [field] * 10 + [
            pltpu.SMEM(perm_table.shape, F32),
            pltpu.SMEM(rate_table.shape, F32),
            coarse,
            coarse,
            pltpu.VMEM((FINE, 8, nz // 2), F32),
            pltpu.VMEM((FINE, S, 8, nz // 2), F32),
            pltpu.VMEM((S, rows, nz), F32),
            pltpu.VMEM((S, rows, nz), F32),
            pltpu.VMEM((S, rows // 2, nz // 2), F32),
            pltpu.VMEM((S, rows // 2, nz // 2), F32),
            coarse,
            coarse,
            dma((8,)),
            dma((S - 1,)), dma((S - 1,)),
            dma((S - 1,)), dma((S - 1,)),
            dma((S - 1, T - 1)), dma((S - 1, T - 1)),
            dma((FINE, S - 1)), dma((FINE, S - 1)),
            dma((S,)), dma((S,)),
            dma((S,)), dma((S,)),
            dma((1,)), dma((1,)),
        ],
        compiler_params=pltpu.CompilerParams(
            collective_id=0, has_side_effects=True, vmem_limit_bytes=40 * 1024 * 1024),
    )(state[0, 0], classes[0], perm_table, rate_table)
    return updated[None, None]


def with_halo(array, sides, width):
    for axis, dim in sides:
        devices, length = (lax.axis_size(axis), array.shape[dim])
        up = [(i, (i + 1) % devices) for i in range(devices)]
        down = [(j, i) for i, j in up]
        last = lax.slice_in_dim(array, length - width, length, axis=dim)
        first = lax.slice_in_dim(array, 0, width, axis=dim)
        before = lax.ppermute(last, axis, up)
        after = lax.ppermute(first, axis, down)
        array = jnp.concatenate([before, array, after], axis=dim)
    return array


def passed_along(array, axis, by):
    devices = lax.axis_size(axis)
    pairs = [(i, i + by) for i in range(devices) if 0 <= i + by < devices]
    return lax.ppermute(array, axis, pairs)


def lookup(table, classes):
    values = jnp.zeros(classes.shape, jnp.float32)
    for entry in range(table.shape[0]):
        values = jnp.where(classes == entry, table[entry], values)
    return values


def restrict(field):
    cx, ny, nz = field.shape
    return field.reshape(cx, ny // 2, 2, nz // 2, 2).mean(axis=(2, 4))


def prolong(coarse):
    return jnp.repeat(jnp.repeat(coarse, 2, axis=1), 2, axis=2)


def vertical(field):
    zero_plane = jnp.zeros(field.shape[:2] + (1,), jnp.float32)
    upper = jnp.concatenate([field[:, :, 1:], zero_plane], axis=2)
    lower = jnp.concatenate([zero_plane, field[:, :, :-1]], axis=2)
    return (upper, lower)


def operate(field):
    padded = with_halo(field, (("space", 0),), 1)
    upper, lower = vertical(field)
    beside = padded[2:] + padded[:-2]
    beside = beside + jnp.roll(field, -1, 1) + jnp.roll(field, 1, 1)
    beside = beside + upper + lower
    return (1.0 + 6.0 * DIFF) * field - DIFF * beside


def squares(residual):
    return lax.psum(jnp.sum(residual * residual), "space")


def fine_step(field, perm):
    upper, lower = vertical(field)
    rhs = field - ADV * perm * field * (upper - lower)
    solution = field
    residual = rhs - operate(solution)
    direction = residual
    norm_now = squares(residual)
    for step in range(ITERS):
        image = operate(direction)
        alpha = norm_now / lax.psum(jnp.sum(direction * image), "space")
        solution = solution + alpha * direction
        residual = residual - alpha * image
        norm_next = squares(residual)
        direction = residual + norm_next / norm_now * direction
        norm_now = norm_next
    return solution


def body(state, classes, perm_table, rate_table):
    start = state[0]
    perm = lookup(perm_table, classes)
    coarse_ratio = 1.0 / (1.0 + restrict(lookup(rate_table, classes)))
    field = start
    for step in range(FINE):
        field = fine_step(field, perm)
    coarse_start = restrict(start)
    jump = field - prolong(coarse_ratio * coarse_start)
    jump_coarse = restrict(jump)
    first = lax.axis_index("tm") == 0
    factor = jnp.where(first, 0.0, coarse_ratio)
    offset = jnp.where(first, coarse_ratio * coarse_start + jump_coarse, jump_coarse)
    before = passed_along(jump, "tm", 1)
    before_coarse = restrict(before)

    def relay_turn(turn, carry):
        outgoing, received = carry
        received = passed_along(outgoing, "tm", 1)
        return (factor * received + offset, received)

    outgoing, received = lax.fori_loop(
        0, lax.axis_size("tm") - 1, relay_turn, (offset, jnp.zeros_like(offset))
    )
    updated = jnp.where(first, start, before + prolong(received - before_coarse))
    return updated[None]


def solution(mesh):
    placed = (
        P(("groups", "tm"), "space", None, None),
        P(("groups", "space"), None, None),
        P(),
        P(),
    )
    devices, slices = (mesh.shape["space"], mesh.shape["tm"])

    def chosen(state, classes, perm_table, rate_table):
        planes, ny, nz = state.shape[1:]
        fits = planes == 1 and ny // devices >= 4 * HALO and nz % 256 == 0
        if fits and slices == 4 and devices >= 3:
            return fused_body(devices, slices, state, classes, perm_table, rate_table)
        return body(state, classes, perm_table, rate_table)

    return jax.shard_map(
        chosen,
        mesh=mesh,
        in_specs=placed,
        out_specs=P(("groups", "tm"), "space", None, None),
        check_vma=False,
    )
```

```python
import functools

import jax
import jax.numpy as jnp
from jax import lax
from jax.experimental import pallas as pl
from jax.experimental.pallas import tpu as pltpu
from jax.sharding import PartitionSpec as P

ITERS = 3
FINE = 2


DIFF = 2.0
ADV = 0.25

CENTRE = 1.0 + 6.0 * DIFF
SCALE = 0.125
BESIDE = DIFF / SCALE
LOWEST = CENTRE - 6.0 * DIFF
HIGHEST = CENTRE + 6.0 * DIFF
HALO = 8
MOMENTS = 2 * ITERS
F32 = jnp.float32
BF16 = jnp.bfloat16


def pieces(value):
    high = value.astype(BF16)
    rest = value - high.astype(F32)
    middle = rest.astype(BF16)
    low = (rest - middle.astype(F32)).astype(BF16)
    return high, middle, low


def times(value, matrix):
    a, b, c = pieces(value)
    dot = functools.partial(jnp.dot, preferred_element_type=F32)
    return dot(a, matrix) + (dot(b, matrix) + dot(c, matrix))


def times_left(matrix, value):
    a, b, c = pieces(value)
    dot = functools.partial(jnp.dot, preferred_element_type=F32)
    return dot(matrix, a) + (dot(matrix, b) + dot(matrix, c))


def pairs(small, large, along, value):
    i = lax.broadcasted_iota(jnp.int32, (small, large) if along else (large, small), 0 if along else 1)
    j = lax.broadcasted_iota(jnp.int32, (small, large) if along else (large, small), 1 if along else 0)
    off = j - 2 * i
    return jnp.where((off == 0) | (off == 1), value, 0.0).astype(BF16)


def restricted(field):
    ny, nz = field.shape
    narrow = times(field, pairs(nz // 2, nz, False, 0.5))
    return times_left(pairs(ny // 2, ny, True, 0.5), narrow)


def prolonged(coarse):
    cy, cz = coarse.shape
    right = pairs(cz, 2 * cz, True, 1.0)
    left = pairs(cy, 2 * cy, False, 1.0)
    dot = functools.partial(jnp.dot, preferred_element_type=F32)
    total = None
    for piece in pieces(coarse):
        wide = dot(left, dot(piece, right).astype(BF16))
        total = wide if total is None else total + wide
    return total


def looked_up(table_ref, classes):
    values = jnp.full(classes.shape, table_ref[0], F32)
    for entry in range(1, table_ref.shape[0]):
        values = jnp.where(classes == entry, table_ref[entry], values)
    return values


def coefficients(moments):
    def inner(a, b):
        total = None
        for i, x in enumerate(a):
            for j, y in enumerate(b):
                term = x * y * moments[i + j]
                total = term if total is None else total + term
        return total

    one = jnp.ones_like(moments[0])
    residual, direction, solution = [one], [one], []
    norm_now = moments[0]
    for step in range(ITERS):
        image = [CENTRE * d for d in direction] + [0.0 * one]
        for i, d in enumerate(direction):
            image[i + 1] = image[i + 1] - BESIDE * d
        alpha = norm_now / inner(direction, image)
        alpha = jnp.clip(alpha, 1.0 / HIGHEST, 1.0 / LOWEST)
        for i, d in enumerate(direction):
            if i < len(solution):
                solution[i] = solution[i] + alpha * d
            else:
                solution.append(alpha * d)
        if step == ITERS - 1:
            break
        residual = residual + [0.0 * one]
        residual = [r - alpha * a for r, a in zip(residual, image)]
        norm_next = inner(residual, residual)
        beta = jnp.clip(norm_next / norm_now, 0.0, HIGHEST - LOWEST)
        direction = [r + beta * d for r, d in zip(residual, direction + [0.0 * one])]
        norm_now = norm_next
    return solution


def kernel(S, T, state_ref, classes_ref, perm_hbm, rate_hbm, out_ref,
           ext, extk, cbuf, kbuf, nbuf, dbuf, w0, w1, w2, w3, d0, d1, d2, perm_buf,
           perm_ref, rate_ref, rs_buf, ratio_buf, msrc, mbuf, jsrc, jbuf, gsrc, gbuf, hsrc, hbuf,
           local_sem, c_send, c_recv, k_send, k_recv, f_send, f_recv, m_send, m_recv,
           j_send, j_recv, g_send, g_recv, h_send, h_recv):
    NY, NZ = state_ref.shape
    rows = NY // S
    slab = rows + 2 * HALO
    own = slice(HALO, HALO + rows)
    me = lax.axis_index("space")
    t = lax.axis_index("tm")

    local = []
    for n, (source, target) in enumerate(((state_ref, ext), (classes_ref, extk))):
        local += [
            pltpu.make_async_copy(source, target.at[pl.ds(HALO, NY)], local_sem.at[3 * n]),
            pltpu.make_async_copy(
                source.at[pl.ds(NY - HALO, HALO)], target.at[pl.ds(0, HALO)], local_sem.at[3 * n + 1]),
            pltpu.make_async_copy(
                source.at[pl.ds(0, HALO)], target.at[pl.ds(HALO + NY, HALO)], local_sem.at[3 * n + 2]),
        ]
    local += [
        pltpu.make_async_copy(perm_hbm, perm_ref, local_sem.at[6]),
        pltpu.make_async_copy(rate_hbm, rate_ref, local_sem.at[7]),
    ]
    for copy in local:
        copy.start()

    barrier = pltpu.get_barrier_semaphore()
    partners = [(dt, dz) for dt in range(T) for dz in range(S) if dz == 0 or dt in (0, 1, T - 1)][1:]
    for dt, dz in partners:
        pl.semaphore_signal(
            barrier, inc=1,
            device_id={"tm": lax.rem(t + dt, T), "space": lax.rem(me + dz, S)},
            device_id_type=pl.DeviceIdType.MESH)
    for copy in local:
        copy.wait()
    pl.semaphore_wait(barrier, len(partners))

    high, wide = slab // 2, NZ // 2
    row_part, lane_part = lax.rem(t, 2), lax.div(t, 2)
    lanes = pl.ds(pl.multiple_of(lane_part * wide, 128), wide)
    quarter_rows = pl.ds(pl.multiple_of(row_part * high, 8), high)

    def class_copy(d):
        to = lax.rem(me + d, S)
        start = pl.multiple_of(to * rows + row_part * high, 8)
        return pltpu.make_async_remote_copy(
            src_ref=extk.at[pl.ds(start, high), lanes],
            dst_ref=kbuf.at[me, quarter_rows, lanes],
            send_sem=k_send.at[d - 1], recv_sem=k_recv.at[d - 1],
            device_id={"space": to}, device_id_type=pl.DeviceIdType.MESH)

    def class_forward(d, e):
        place = kbuf.at[lax.rem(me + S - d, S), quarter_rows, lanes]
        return pltpu.make_async_remote_copy(
            src_ref=place, dst_ref=place,
            send_sem=f_send.at[d - 1, e - 1], recv_sem=f_recv.at[d - 1, e - 1],
            device_id={"tm": lax.rem(t + e, T)}, device_id_type=pl.DeviceIdType.MESH)

    def slab_copy(d):
        to = lax.rem(me + d, S)
        return pltpu.make_async_remote_copy(
            src_ref=ext.at[pl.ds(pl.multiple_of(to * rows, 8), slab)],
            dst_ref=cbuf.at[me],
            send_sem=c_send.at[d - 1], recv_sem=c_recv.at[d - 1],
            device_id={"space": to}, device_id_type=pl.DeviceIdType.MESH)

    k_copies = [class_copy(d) for d in range(1, S)]
    c_copies = [slab_copy(d) for d in range(1, S)]
    f_copies = [class_forward(d, e) for d in range(1, S) for e in range(1, T)]
    for copy in k_copies:
        copy.start()
    for copy in c_copies:
        copy.start()
    mine = pl.ds(pl.multiple_of(me * rows, 8), slab)
    cbuf[me] = ext[mine]
    kbuf[me] = extk[mine]

    @pl.when(t == 0)
    def _():
        out_ref[...] = ext[HALO:HALO + NY]

    for d in range(1, S):
        k_copies[d - 1].wait_recv()
        for e in range(1, T):
            f_copies[(d - 1) * (T - 1) + e - 1].start()

    i = lax.broadcasted_iota(jnp.int32, (NZ, NZ), 0)
    j = lax.broadcasted_iota(jnp.int32, (NZ, NZ), 1)
    up, down = i - j == 1, j - i == 1
    both = jnp.where(up | down, 1.0, 0.0).astype(BF16)
    apart = jnp.where(up, 1.0, jnp.where(down, -1.0, 0.0)).astype(BF16)

    def neighbours(ref, p):
        value = ref[p]
        total = times(value, both)
        total = total + (ref[(p + 1) % S] + ref[(p + S - 1) % S])
        total = total + (pltpu.roll(value, 1, 0) + pltpu.roll(value, slab - 1, 0))
        return SCALE * total

    def dot_rows(a, b):
        product = (a * b)[own]
        return product.reshape(rows // 8, 8, NZ).sum(axis=0)

    for copy in c_copies:
        copy.wait_recv()
    for p in range(S):
        nbuf[p] = neighbours(cbuf, p)
        dbuf[p] = times(cbuf[p], apart)
    for copy in f_copies:
        copy.wait_recv()
    for p in range(S):
        c = cbuf[p]
        perm = looked_up(perm_ref, kbuf[p])
        perm_buf[p] = perm
        w0[p] = c - ADV * perm * c * dbuf[p] - CENTRE * c + BESIDE * nbuf[p]

    def arriving(source, target, send, recv, p):
        return pltpu.make_async_remote_copy(
            src_ref=source, dst_ref=target, send_sem=send, recv_sem=recv,
            device_id={"tm": lax.rem(t + 1, T), "space": p}, device_id_type=pl.DeviceIdType.MESH)

    def jump_copy(p):
        return arriving(jsrc.at[p], jbuf.at[me], j_send.at[p], j_recv.at[me], p)

    def coarse_copy(p):
        return arriving(gsrc.at[p], gbuf.at[me], g_send.at[p], g_recv.at[me], p)

    chain_copy = arriving(hsrc, hbuf, h_send.at[0], h_recv.at[0], me)

    krylov = (w0, w1, w2, w3)
    for fine in range(FINE):
        sums = [None] * MOMENTS
        for k in range(ITERS):
            source, target = krylov[k], krylov[k + 1]
            for p in range(S):
                value = neighbours(source, p)
                target[p] = value
                here = source[p]
                for order, term in ((2 * k, dot_rows(here, here)), (2 * k + 1, dot_rows(here, value))):
                    sums[order] = term if sums[order] is None else sums[order] + term
        lines = [jnp.sum(s[:, :NZ // 2] + s[:, NZ // 2:], axis=0, keepdims=True) for s in sums]
        lines = lines + [jnp.zeros_like(lines[0])] * (8 - MOMENTS)
        msrc[fine] = jnp.concatenate(lines, axis=0)
        mbuf[fine, me] = msrc[fine]
        m_copies = [
            pltpu.make_async_remote_copy(
                src_ref=msrc.at[fine], dst_ref=mbuf.at[fine, me],
                send_sem=m_send.at[fine, d - 1], recv_sem=m_recv.at[fine, d - 1],
                device_id={"space": lax.rem(me + d, S)}, device_id_type=pl.DeviceIdType.MESH)
            for d in range(1, S)
        ]
        for copy in m_copies:
            copy.start()
        if fine < FINE - 1:
            for p in range(S):
                d0[p] = times(w0[p], apart)
                d1[p] = times(w1[p], apart)
                d2[p] = times(w2[p], apart)
        if fine == 0:
            whole = jnp.concatenate([cbuf[p][own] for p in range(S)], axis=0)
            kinds = jnp.concatenate([kbuf[p][own] for p in range(S)], axis=0)
            ratio_buf[...] = 1.0 / (1.0 + restricted(looked_up(rate_ref, kinds)))
            rs_buf[...] = restricted(whole)
        for copy in m_copies:
            copy.wait()
        total = mbuf[fine, 0]
        for d in range(1, S):
            total = total + mbuf[fine, d]
        total = jnp.sum(total, axis=1, keepdims=True)
        found = [jnp.broadcast_to(total[k:k + 1, :], (1, NZ)) for k in range(MOMENTS)]
        a = coefficients(found)
        if fine < FINE - 1:
            for p in range(S):
                x0, x1, x2, x3 = w0[p], w1[p], w2[p], w3[p]
                c = cbuf[p] + a[0] * x0 + a[1] * x1 + a[2] * x2
                near = nbuf[p] + a[0] * x1 + a[1] * x2 + a[2] * x3
                apart_c = dbuf[p] + a[0] * d0[p] + a[1] * d1[p] + a[2] * d2[p]
                cbuf[p] = c
                nbuf[p] = near
                dbuf[p] = apart_c
                w0[p] = c - ADV * perm_buf[p] * c * apart_c - CENTRE * c + BESIDE * near
        else:
            for p in range(S):
                jsrc[p] = cbuf[p][own] + (a[0] * w0[p][own] + a[1] * w1[p][own] + a[2] * w2[p][own])

                @pl.when(t < T - 1)
                def _():
                    jump_copy(p).start()

    @pl.when(t < T - 2)
    def _():
        hsrc[...] = restricted(jsrc[...].reshape(NY, NZ))

    @pl.when((t > 0) & (t < T - 1))
    def _():
        chain_copy.wait_recv()
        correction = ratio_buf[...] * (hbuf[...] - rs_buf[...])
        gsrc[...] = correction.reshape(S, rows // 2, NZ // 2)

    @pl.when((t > 0) & (t < T - 2))
    def _():
        hsrc[...] += gsrc[...].reshape(NY // 2, NZ // 2)

    @pl.when(t < T - 2)
    def _():
        chain_copy.start()

    @pl.when((t > 0) & (t < T - 1))
    def _():
        for p in range(S):
            coarse_copy(p).start()

    @pl.when(t > 1)
    def _():
        for p in range(S):
            arriving(gsrc.at[p], gbuf.at[p], g_send.at[p], g_recv.at[p], p).wait_recv()
        out_ref[...] = prolonged(gbuf[...].reshape(NY // 2, NZ // 2))

    @pl.when(t == 1)
    def _():
        out_ref[...] = jnp.zeros_like(out_ref)

    @pl.when(t > 0)
    def _():
        for p in range(S):
            arriving(jsrc.at[p], jbuf.at[p], j_send.at[p], j_recv.at[p], p).wait_recv()
        out_ref[...] += jbuf[...].reshape(NY, NZ)

    for copy in c_copies + k_copies + f_copies:
        copy.wait_send()

    @pl.when(t < T - 1)
    def _():
        for p in range(S):
            jump_copy(p).wait_send()

    @pl.when(t < T - 2)
    def _():
        chain_copy.wait_send()

    @pl.when((t > 0) & (t < T - 1))
    def _():
        for p in range(S):
            coarse_copy(p).wait_send()


def fused_body(S, T, state, classes, perm_table, rate_table):
    ny, nz = state.shape[2:]
    rows = ny // S
    slab = rows + 2 * HALO
    field = pltpu.VMEM((S, slab, nz), F32)
    coarse = pltpu.VMEM((ny // 2, nz // 2), F32)
    dma = pltpu.SemaphoreType.DMA
    updated = pl.pallas_call(
        functools.partial(kernel, S, T),
        out_shape=jax.ShapeDtypeStruct((ny, nz), F32),
        in_specs=[pl.BlockSpec(memory_space=pltpu.HBM)] * 4,
        out_specs=pl.BlockSpec(memory_space=pltpu.VMEM),
        scratch_shapes=[
            pltpu.VMEM((ny + 2 * HALO, nz), F32),
            pltpu.VMEM((ny + 2 * HALO, nz), jnp.int32),
            field,
            pltpu.VMEM((S, slab, nz), jnp.int32),
        ] + [field] * 10 + [
            pltpu.SMEM(perm_table.shape, F32),
            pltpu.SMEM(rate_table.shape, F32),
            coarse,
            coarse,
            pltpu.VMEM((FINE, 8, nz // 2), F32),
            pltpu.VMEM((FINE, S, 8, nz // 2), F32),
            pltpu.VMEM((S, rows, nz), F32),
            pltpu.VMEM((S, rows, nz), F32),
            pltpu.VMEM((S, rows // 2, nz // 2), F32),
            pltpu.VMEM((S, rows // 2, nz // 2), F32),
            coarse,
            coarse,
            dma((8,)),
            dma((S - 1,)), dma((S - 1,)),
            dma((S - 1,)), dma((S - 1,)),
            dma((S - 1, T - 1)), dma((S - 1, T - 1)),
            dma((FINE, S - 1)), dma((FINE, S - 1)),
            dma((S,)), dma((S,)),
            dma((S,)), dma((S,)),
            dma((1,)), dma((1,)),
        ],
        compiler_params=pltpu.CompilerParams(
            collective_id=0, has_side_effects=True, vmem_limit_bytes=56 * 1024 * 1024),
    )(state[0, 0], classes[0], perm_table, rate_table)
    return updated[None, None]


def with_halo(array, sides, width):
    for axis, dim in sides:
        devices, length = (lax.axis_size(axis), array.shape[dim])
        up = [(i, (i + 1) % devices) for i in range(devices)]
        down = [(j, i) for i, j in up]
        last = lax.slice_in_dim(array, length - width, length, axis=dim)
        first = lax.slice_in_dim(array, 0, width, axis=dim)
        before = lax.ppermute(last, axis, up)
        after = lax.ppermute(first, axis, down)
        array = jnp.concatenate([before, array, after], axis=dim)
    return array


def passed_along(array, axis, by):
    devices = lax.axis_size(axis)
    pairs = [(i, i + by) for i in range(devices) if 0 <= i + by < devices]
    return lax.ppermute(array, axis, pairs)


def lookup(table, classes):
    values = jnp.zeros(classes.shape, jnp.float32)
    for entry in range(table.shape[0]):
        values = jnp.where(classes == entry, table[entry], values)
    return values


def restrict(field):
    cx, ny, nz = field.shape
    return field.reshape(cx, ny // 2, 2, nz // 2, 2).mean(axis=(2, 4))


def prolong(coarse):
    return jnp.repeat(jnp.repeat(coarse, 2, axis=1), 2, axis=2)


def vertical(field):
    zero_plane = jnp.zeros(field.shape[:2] + (1,), jnp.float32)
    upper = jnp.concatenate([field[:, :, 1:], zero_plane], axis=2)
    lower = jnp.concatenate([zero_plane, field[:, :, :-1]], axis=2)
    return (upper, lower)


def operate(field):
    padded = with_halo(field, (("space", 0),), 1)
    upper, lower = vertical(field)
    beside = padded[2:] + padded[:-2]
    beside = beside + jnp.roll(field, -1, 1) + jnp.roll(field, 1, 1)
    beside = beside + upper + lower
    return (1.0 + 6.0 * DIFF) * field - DIFF * beside


def squares(residual):
    return lax.psum(jnp.sum(residual * residual), "space")


def fine_step(field, perm):
    upper, lower = vertical(field)
    rhs = field - ADV * perm * field * (upper - lower)
    solution = field
    residual = rhs - operate(solution)
    direction = residual
    norm_now = squares(residual)
    for step in range(ITERS):
        image = operate(direction)
        alpha = norm_now / lax.psum(jnp.sum(direction * image), "space")
        solution = solution + alpha * direction
        residual = residual - alpha * image
        norm_next = squares(residual)
        direction = residual + norm_next / norm_now * direction
        norm_now = norm_next
    return solution


def body(state, classes, perm_table, rate_table):
    start = state[0]
    perm = lookup(perm_table, classes)
    coarse_ratio = 1.0 / (1.0 + restrict(lookup(rate_table, classes)))
    field = start
    for step in range(FINE):
        field = fine_step(field, perm)
    coarse_start = restrict(start)
    jump = field - prolong(coarse_ratio * coarse_start)
    jump_coarse = restrict(jump)
    first = lax.axis_index("tm") == 0
    factor = jnp.where(first, 0.0, coarse_ratio)
    offset = jnp.where(first, coarse_ratio * coarse_start + jump_coarse, jump_coarse)
    before = passed_along(jump, "tm", 1)
    before_coarse = restrict(before)

    def relay_turn(turn, carry):
        outgoing, received = carry
        received = passed_along(outgoing, "tm", 1)
        return (factor * received + offset, received)

    outgoing, received = lax.fori_loop(
        0, lax.axis_size("tm") - 1, relay_turn, (offset, jnp.zeros_like(offset))
    )
    updated = jnp.where(first, start, before + prolong(received - before_coarse))
    return updated[None]


def solution(mesh):
    placed = (
        P(("groups", "tm"), "space", None, None),
        P(("groups", "space"), None, None),
        P(),
        P(),
    )
    devices, slices = (mesh.shape["space"], mesh.shape["tm"])

    def chosen(state, classes, perm_table, rate_table):
        planes, ny, nz = state.shape[1:]
        fits = planes == 1 and ny // devices >= 4 * HALO and nz % 256 == 0
        if fits and slices == 4 and devices >= 3:
            return fused_body(devices, slices, state, classes, perm_table, rate_table)
        return body(state, classes, perm_table, rate_table)

    return jax.shard_map(
        chosen,
        mesh=mesh,
        in_specs=placed,
        out_specs=P(("groups", "tm"), "space", None, None),
        check_vma=False,
    )
```

```python
import functools

import jax
import jax.numpy as jnp
from jax import lax
from jax.experimental import pallas as pl
from jax.experimental.pallas import tpu as pltpu
from jax.sharding import PartitionSpec as P

ITERS = 3
FINE = 2


DIFF = 2.0
ADV = 0.25

CENTRE = 1.0 + 6.0 * DIFF
SCALE = 0.125
BESIDE = DIFF / SCALE
LOWEST = CENTRE - 6.0 * DIFF
HIGHEST = CENTRE + 6.0 * DIFF
HALO = 8
MOMENTS = 2 * ITERS
F32 = jnp.float32
BF16 = jnp.bfloat16


def pieces(value):
    high = value.astype(BF16)
    rest = value - high.astype(F32)
    middle = rest.astype(BF16)
    low = (rest - middle.astype(F32)).astype(BF16)
    return high, middle, low


def times(value, matrix):
    a, b, c = pieces(value)
    dot = functools.partial(jnp.dot, preferred_element_type=F32)
    return dot(a, matrix) + (dot(b, matrix) + dot(c, matrix))


def times_left(matrix, value):
    a, b, c = pieces(value)
    dot = functools.partial(jnp.dot, preferred_element_type=F32)
    return dot(matrix, a) + (dot(matrix, b) + dot(matrix, c))


def pairs(small, large, along, value):
    i = lax.broadcasted_iota(jnp.int32, (small, large) if along else (large, small), 0 if along else 1)
    j = lax.broadcasted_iota(jnp.int32, (small, large) if along else (large, small), 1 if along else 0)
    off = j - 2 * i
    return jnp.where((off == 0) | (off == 1), value, 0.0).astype(BF16)


def restricted(field):
    ny, nz = field.shape
    narrow = times(field, pairs(nz // 2, nz, False, 0.5))
    return times_left(pairs(ny // 2, ny, True, 0.5), narrow)


def prolonged(coarse):
    cy, cz = coarse.shape
    right = pairs(cz, 2 * cz, True, 1.0)
    left = pairs(cy, 2 * cy, False, 1.0)
    dot = functools.partial(jnp.dot, preferred_element_type=F32)
    total = None
    for piece in pieces(coarse):
        wide = dot(left, dot(piece, right).astype(BF16))
        total = wide if total is None else total + wide
    return total


def looked_up(table_ref, classes):
    values = jnp.full(classes.shape, table_ref[0], F32)
    for entry in range(1, table_ref.shape[0]):
        values = jnp.where(classes == entry, table_ref[entry], values)
    return values


def coefficients(moments):
    def inner(a, b):
        total = None
        for i, x in enumerate(a):
            for j, y in enumerate(b):
                term = x * y * moments[i + j]
                total = term if total is None else total + term
        return total

    one = jnp.ones_like(moments[0])
    residual, direction, solution = [one], [one], []
    norm_now = moments[0]
    for step in range(ITERS):
        image = [CENTRE * d for d in direction] + [0.0 * one]
        for i, d in enumerate(direction):
            image[i + 1] = image[i + 1] - BESIDE * d
        alpha = norm_now / inner(direction, image)
        alpha = jnp.clip(alpha, 1.0 / HIGHEST, 1.0 / LOWEST)
        for i, d in enumerate(direction):
            if i < len(solution):
                solution[i] = solution[i] + alpha * d
            else:
                solution.append(alpha * d)
        if step == ITERS - 1:
            break
        residual = residual + [0.0 * one]
        residual = [r - alpha * a for r, a in zip(residual, image)]
        norm_next = inner(residual, residual)
        beta = jnp.clip(norm_next / norm_now, 0.0, HIGHEST - LOWEST)
        direction = [r + beta * d for r, d in zip(residual, direction + [0.0 * one])]
        norm_now = norm_next
    return solution


def kernel(S, T, state_ref, classes_ref, perm_hbm, rate_hbm, out_ref,
           ext, extk, cbuf, kbuf, nbuf, dbuf, w0, w1, w2, w3, d0, d1, d2, perm_buf,
           perm_ref, rate_ref, rs_buf, ratio_buf, msrc, mbuf, jsrc, jbuf, gsrc, gbuf, hsrc, hbuf,
           local_sem, c_send, c_recv, k_send, k_recv, f_send, f_recv, m_send, m_recv,
           j_send, j_recv, g_send, g_recv, h_send, h_recv):
    NY, NZ = state_ref.shape
    rows = NY // S
    slab = rows + 2 * HALO
    own = slice(HALO, HALO + rows)
    me = lax.axis_index("space")
    t = lax.axis_index("tm")

    local = []
    for n, (source, target) in enumerate(((state_ref, ext), (classes_ref, extk))):
        local += [
            pltpu.make_async_copy(source, target.at[pl.ds(HALO, NY)], local_sem.at[3 * n]),
            pltpu.make_async_copy(
                source.at[pl.ds(NY - HALO, HALO)], target.at[pl.ds(0, HALO)], local_sem.at[3 * n + 1]),
            pltpu.make_async_copy(
                source.at[pl.ds(0, HALO)], target.at[pl.ds(HALO + NY, HALO)], local_sem.at[3 * n + 2]),
        ]
    local += [
        pltpu.make_async_copy(perm_hbm, perm_ref, local_sem.at[6]),
        pltpu.make_async_copy(rate_hbm, rate_ref, local_sem.at[7]),
    ]
    for copy in local:
        copy.start()

    barrier = pltpu.get_barrier_semaphore()
    partners = [(dt, dz) for dt in range(T) for dz in range(S) if dz == 0 or dt in (0, 1, T - 1)][1:]
    for dt, dz in partners:
        pl.semaphore_signal(
            barrier, inc=1,
            device_id={"tm": lax.rem(t + dt, T), "space": lax.rem(me + dz, S)},
            device_id_type=pl.DeviceIdType.MESH)
    for copy in local:
        copy.wait()
    pl.semaphore_wait(barrier, len(partners))

    high, wide = slab // 2, NZ // 2
    row_part, lane_part = lax.rem(t, 2), lax.div(t, 2)
    lanes = pl.ds(pl.multiple_of(lane_part * wide, 128), wide)
    quarter_rows = pl.ds(pl.multiple_of(row_part * high, 8), high)

    def class_copy(d):
        to = lax.rem(me + d, S)
        start = pl.multiple_of(to * rows + row_part * high, 8)
        return pltpu.make_async_remote_copy(
            src_ref=extk.at[pl.ds(start, high), lanes],
            dst_ref=kbuf.at[me, quarter_rows, lanes],
            send_sem=k_send.at[d - 1], recv_sem=k_recv.at[d - 1],
            device_id={"space": to}, device_id_type=pl.DeviceIdType.MESH)

    def class_forward(d, e):
        place = kbuf.at[lax.rem(me + S - d, S), quarter_rows, lanes]
        return pltpu.make_async_remote_copy(
            src_ref=place, dst_ref=place,
            send_sem=f_send.at[d - 1, e - 1], recv_sem=f_recv.at[d - 1, e - 1],
            device_id={"tm": lax.rem(t + e, T)}, device_id_type=pl.DeviceIdType.MESH)

    def slab_copy(d):
        to = lax.rem(me + d, S)
        return pltpu.make_async_remote_copy(
            src_ref=ext.at[pl.ds(pl.multiple_of(to * rows, 8), slab)],
            dst_ref=cbuf.at[me],
            send_sem=c_send.at[d - 1], recv_sem=c_recv.at[d - 1],
            device_id={"space": to}, device_id_type=pl.DeviceIdType.MESH)

    k_copies = [class_copy(d) for d in range(1, S)]
    c_copies = [slab_copy(d) for d in range(1, S)]
    f_copies = [class_forward(d, e) for d in range(1, S) for e in range(1, T)]
    for copy in k_copies:
        copy.start()
    for copy in c_copies:
        copy.start()
    mine = pl.ds(pl.multiple_of(me * rows, 8), slab)
    cbuf[me] = ext[mine]
    kbuf[me] = extk[mine]

    @pl.when(t == 0)
    def _():
        out_ref[...] = ext[HALO:HALO + NY]

    for d in range(1, S):
        k_copies[d - 1].wait_recv()
        for e in range(1, T):
            f_copies[(d - 1) * (T - 1) + e - 1].start()

    lane = lax.broadcasted_iota(jnp.int32, (slab, NZ), 1)

    def vertical_pair(value):
        upper = jnp.where(lane == NZ - 1, 0.0, pltpu.roll(value, NZ - 1, 1))
        lower = jnp.where(lane == 0, 0.0, pltpu.roll(value, 1, 1))
        return upper, lower

    def apart(value):
        upper, lower = vertical_pair(value)
        return upper - lower

    def neighbours(ref, p):
        value = ref[p]
        upper, lower = vertical_pair(value)
        total = (upper + lower) + (ref[(p + 1) % S] + ref[(p + S - 1) % S])
        total = total + (pltpu.roll(value, 1, 0) + pltpu.roll(value, slab - 1, 0))
        return SCALE * total

    def dot_rows(a, b):
        product = (a * b)[own]
        return product.reshape(rows // 8, 8, NZ).sum(axis=0)

    for copy in c_copies:
        copy.wait_recv()
    for p in range(S):
        nbuf[p] = neighbours(cbuf, p)
        dbuf[p] = apart(cbuf[p])
    for copy in f_copies:
        copy.wait_recv()
    for p in range(S):
        c = cbuf[p]
        perm = looked_up(perm_ref, kbuf[p])
        perm_buf[p] = perm
        w0[p] = c - ADV * perm * c * dbuf[p] - CENTRE * c + BESIDE * nbuf[p]

    def arriving(source, target, send, recv, p):
        return pltpu.make_async_remote_copy(
            src_ref=source, dst_ref=target, send_sem=send, recv_sem=recv,
            device_id={"tm": lax.rem(t + 1, T), "space": p}, device_id_type=pl.DeviceIdType.MESH)

    def jump_copy(p):
        return arriving(jsrc.at[p], jbuf.at[me], j_send.at[p], j_recv.at[me], p)

    def coarse_copy(p):
        return arriving(gsrc.at[p], gbuf.at[me], g_send.at[p], g_recv.at[me], p)

    chain_copy = arriving(hsrc, hbuf, h_send.at[0], h_recv.at[0], me)

    krylov = (w0, w1, w2, w3)
    for fine in range(FINE):
        sums = [None] * MOMENTS
        for k in range(ITERS):
            source, target = krylov[k], krylov[k + 1]
            for p in range(S):
                value = neighbours(source, p)
                target[p] = value
                here = source[p]
                for order, term in ((2 * k, dot_rows(here, here)), (2 * k + 1, dot_rows(here, value))):
                    sums[order] = term if sums[order] is None else sums[order] + term
        lines = [jnp.sum(s[:, :NZ // 2] + s[:, NZ // 2:], axis=0, keepdims=True) for s in sums]
        lines = lines + [jnp.zeros_like(lines[0])] * (8 - MOMENTS)
        msrc[fine] = jnp.concatenate(lines, axis=0)
        mbuf[fine, me] = msrc[fine]
        m_copies = [
            pltpu.make_async_remote_copy(
                src_ref=msrc.at[fine], dst_ref=mbuf.at[fine, me],
                send_sem=m_send.at[fine, d - 1], recv_sem=m_recv.at[fine, d - 1],
                device_id={"space": lax.rem(me + d, S)}, device_id_type=pl.DeviceIdType.MESH)
            for d in range(1, S)
        ]
        for copy in m_copies:
            copy.start()
        if fine < FINE - 1:
            for p in range(S):
                d0[p] = apart(w0[p])
                d1[p] = apart(w1[p])
                d2[p] = apart(w2[p])
        if fine == 0:
            whole = jnp.concatenate([cbuf[p][own] for p in range(S)], axis=0)
            kinds = jnp.concatenate([kbuf[p][own] for p in range(S)], axis=0)
            ratio_buf[...] = 1.0 / (1.0 + restricted(looked_up(rate_ref, kinds)))
            rs_buf[...] = restricted(whole)
        for copy in m_copies:
            copy.wait()
        total = mbuf[fine, 0]
        for d in range(1, S):
            total = total + mbuf[fine, d]
        total = jnp.sum(total, axis=1, keepdims=True)
        found = [jnp.broadcast_to(total[k:k + 1, :], (1, NZ)) for k in range(MOMENTS)]
        a = coefficients(found)
        if fine < FINE - 1:
            for p in range(S):
                x0, x1, x2, x3 = w0[p], w1[p], w2[p], w3[p]
                c = cbuf[p] + a[0] * x0 + a[1] * x1 + a[2] * x2
                near = nbuf[p] + a[0] * x1 + a[1] * x2 + a[2] * x3
                apart_c = dbuf[p] + a[0] * d0[p] + a[1] * d1[p] + a[2] * d2[p]
                cbuf[p] = c
                nbuf[p] = near
                dbuf[p] = apart_c
                w0[p] = c - ADV * perm_buf[p] * c * apart_c - CENTRE * c + BESIDE * near
        else:
            for p in range(S):
                jsrc[p] = cbuf[p][own] + (a[0] * w0[p][own] + a[1] * w1[p][own] + a[2] * w2[p][own])

                @pl.when(t < T - 1)
                def _():
                    jump_copy(p).start()

    @pl.when(t < T - 2)
    def _():
        hsrc[...] = restricted(jsrc[...].reshape(NY, NZ))

    @pl.when((t > 0) & (t < T - 1))
    def _():
        chain_copy.wait_recv()
        correction = ratio_buf[...] * (hbuf[...] - rs_buf[...])
        gsrc[...] = correction.reshape(S, rows // 2, NZ // 2)

    @pl.when((t > 0) & (t < T - 2))
    def _():
        hsrc[...] += gsrc[...].reshape(NY // 2, NZ // 2)

    @pl.when(t < T - 2)
    def _():
        chain_copy.start()

    @pl.when((t > 0) & (t < T - 1))
    def _():
        for p in range(S):
            coarse_copy(p).start()

    @pl.when(t > 1)
    def _():
        for p in range(S):
            arriving(gsrc.at[p], gbuf.at[p], g_send.at[p], g_recv.at[p], p).wait_recv()
        out_ref[...] = prolonged(gbuf[...].reshape(NY // 2, NZ // 2))

    @pl.when(t == 1)
    def _():
        out_ref[...] = jnp.zeros_like(out_ref)

    @pl.when(t > 0)
    def _():
        for p in range(S):
            arriving(jsrc.at[p], jbuf.at[p], j_send.at[p], j_recv.at[p], p).wait_recv()
        out_ref[...] += jbuf[...].reshape(NY, NZ)

    for copy in c_copies + k_copies + f_copies:
        copy.wait_send()

    @pl.when(t < T - 1)
    def _():
        for p in range(S):
            jump_copy(p).wait_send()

    @pl.when(t < T - 2)
    def _():
        chain_copy.wait_send()

    @pl.when((t > 0) & (t < T - 1))
    def _():
        for p in range(S):
            coarse_copy(p).wait_send()


def fused_body(S, T, state, classes, perm_table, rate_table):
    ny, nz = state.shape[2:]
    rows = ny // S
    slab = rows + 2 * HALO
    field = pltpu.VMEM((S, slab, nz), F32)
    coarse = pltpu.VMEM((ny // 2, nz // 2), F32)
    dma = pltpu.SemaphoreType.DMA
    updated = pl.pallas_call(
        functools.partial(kernel, S, T),
        out_shape=jax.ShapeDtypeStruct((ny, nz), F32),
        in_specs=[pl.BlockSpec(memory_space=pltpu.HBM)] * 4,
        out_specs=pl.BlockSpec(memory_space=pltpu.VMEM),
        scratch_shapes=[
            pltpu.VMEM((ny + 2 * HALO, nz), F32),
            pltpu.VMEM((ny + 2 * HALO, nz), jnp.int32),
            field,
            pltpu.VMEM((S, slab, nz), jnp.int32),
        ] + [field] * 10 + [
            pltpu.SMEM(perm_table.shape, F32),
            pltpu.SMEM(rate_table.shape, F32),
            coarse,
            coarse,
            pltpu.VMEM((FINE, 8, nz // 2), F32),
            pltpu.VMEM((FINE, S, 8, nz // 2), F32),
            pltpu.VMEM((S, rows, nz), F32),
            pltpu.VMEM((S, rows, nz), F32),
            pltpu.VMEM((S, rows // 2, nz // 2), F32),
            pltpu.VMEM((S, rows // 2, nz // 2), F32),
            coarse,
            coarse,
            dma((8,)),
            dma((S - 1,)), dma((S - 1,)),
            dma((S - 1,)), dma((S - 1,)),
            dma((S - 1, T - 1)), dma((S - 1, T - 1)),
            dma((FINE, S - 1)), dma((FINE, S - 1)),
            dma((S,)), dma((S,)),
            dma((S,)), dma((S,)),
            dma((1,)), dma((1,)),
        ],
        compiler_params=pltpu.CompilerParams(
            collective_id=0, has_side_effects=True, vmem_limit_bytes=56 * 1024 * 1024),
    )(state[0, 0], classes[0], perm_table, rate_table)
    return updated[None, None]


def with_halo(array, sides, width):
    for axis, dim in sides:
        devices, length = (lax.axis_size(axis), array.shape[dim])
        up = [(i, (i + 1) % devices) for i in range(devices)]
        down = [(j, i) for i, j in up]
        last = lax.slice_in_dim(array, length - width, length, axis=dim)
        first = lax.slice_in_dim(array, 0, width, axis=dim)
        before = lax.ppermute(last, axis, up)
        after = lax.ppermute(first, axis, down)
        array = jnp.concatenate([before, array, after], axis=dim)
    return array


def passed_along(array, axis, by):
    devices = lax.axis_size(axis)
    pairs = [(i, i + by) for i in range(devices) if 0 <= i + by < devices]
    return lax.ppermute(array, axis, pairs)


def lookup(table, classes):
    values = jnp.zeros(classes.shape, jnp.float32)
    for entry in range(table.shape[0]):
        values = jnp.where(classes == entry, table[entry], values)
    return values


def restrict(field):
    cx, ny, nz = field.shape
    return field.reshape(cx, ny // 2, 2, nz // 2, 2).mean(axis=(2, 4))


def prolong(coarse):
    return jnp.repeat(jnp.repeat(coarse, 2, axis=1), 2, axis=2)


def vertical(field):
    zero_plane = jnp.zeros(field.shape[:2] + (1,), jnp.float32)
    upper = jnp.concatenate([field[:, :, 1:], zero_plane], axis=2)
    lower = jnp.concatenate([zero_plane, field[:, :, :-1]], axis=2)
    return (upper, lower)


def operate(field):
    padded = with_halo(field, (("space", 0),), 1)
    upper, lower = vertical(field)
    beside = padded[2:] + padded[:-2]
    beside = beside + jnp.roll(field, -1, 1) + jnp.roll(field, 1, 1)
    beside = beside + upper + lower
    return (1.0 + 6.0 * DIFF) * field - DIFF * beside


def squares(residual):
    return lax.psum(jnp.sum(residual * residual), "space")


def fine_step(field, perm):
    upper, lower = vertical(field)
    rhs = field - ADV * perm * field * (upper - lower)
    solution = field
    residual = rhs - operate(solution)
    direction = residual
    norm_now = squares(residual)
    for step in range(ITERS):
        image = operate(direction)
        alpha = norm_now / lax.psum(jnp.sum(direction * image), "space")
        solution = solution + alpha * direction
        residual = residual - alpha * image
        norm_next = squares(residual)
        direction = residual + norm_next / norm_now * direction
        norm_now = norm_next
    return solution


def body(state, classes, perm_table, rate_table):
    start = state[0]
    perm = lookup(perm_table, classes)
    coarse_ratio = 1.0 / (1.0 + restrict(lookup(rate_table, classes)))
    field = start
    for step in range(FINE):
        field = fine_step(field, perm)
    coarse_start = restrict(start)
    jump = field - prolong(coarse_ratio * coarse_start)
    jump_coarse = restrict(jump)
    first = lax.axis_index("tm") == 0
    factor = jnp.where(first, 0.0, coarse_ratio)
    offset = jnp.where(first, coarse_ratio * coarse_start + jump_coarse, jump_coarse)
    before = passed_along(jump, "tm", 1)
    before_coarse = restrict(before)

    def relay_turn(turn, carry):
        outgoing, received = carry
        received = passed_along(outgoing, "tm", 1)
        return (factor * received + offset, received)

    outgoing, received = lax.fori_loop(
        0, lax.axis_size("tm") - 1, relay_turn, (offset, jnp.zeros_like(offset))
    )
    updated = jnp.where(first, start, before + prolong(received - before_coarse))
    return updated[None]


def solution(mesh):
    placed = (
        P(("groups", "tm"), "space", None, None),
        P(("groups", "space"), None, None),
        P(),
        P(),
    )
    devices, slices = (mesh.shape["space"], mesh.shape["tm"])

    def chosen(state, classes, perm_table, rate_table):
        planes, ny, nz = state.shape[1:]
        fits = planes == 1 and ny // devices >= 4 * HALO and nz % 256 == 0
        if fits and slices == 4 and devices >= 3:
            return fused_body(devices, slices, state, classes, perm_table, rate_table)
        return body(state, classes, perm_table, rate_table)

    return jax.shard_map(
        chosen,
        mesh=mesh,
        in_specs=placed,
        out_specs=P(("groups", "tm"), "space", None, None),
        check_vma=False,
    )
```

```python
import functools

import jax
import jax.numpy as jnp
from jax import lax
from jax.experimental import pallas as pl
from jax.experimental.pallas import tpu as pltpu
from jax.sharding import PartitionSpec as P

ITERS = 3
FINE = 2


DIFF = 2.0
ADV = 0.25

CENTRE = 1.0 + 6.0 * DIFF
SCALE = 0.125
BESIDE = DIFF / SCALE
LOWEST = CENTRE - 6.0 * DIFF
HIGHEST = CENTRE + 6.0 * DIFF
HALO = 8
MOMENTS = 2 * ITERS
F32 = jnp.float32
BF16 = jnp.bfloat16


def pieces(value):
    high = value.astype(BF16)
    rest = value - high.astype(F32)
    middle = rest.astype(BF16)
    low = (rest - middle.astype(F32)).astype(BF16)
    return high, middle, low


def times(value, matrix):
    a, b, c = pieces(value)
    dot = functools.partial(jnp.dot, preferred_element_type=F32)
    return dot(a, matrix) + (dot(b, matrix) + dot(c, matrix))


def times_left(matrix, value):
    a, b, c = pieces(value)
    dot = functools.partial(jnp.dot, preferred_element_type=F32)
    return dot(matrix, a) + (dot(matrix, b) + dot(matrix, c))


def pairs(small, large, along, value):
    i = lax.broadcasted_iota(jnp.int32, (small, large) if along else (large, small), 0 if along else 1)
    j = lax.broadcasted_iota(jnp.int32, (small, large) if along else (large, small), 1 if along else 0)
    off = j - 2 * i
    return jnp.where((off == 0) | (off == 1), value, 0.0).astype(BF16)


def restricted(field):
    ny, nz = field.shape
    narrow = times(field, pairs(nz // 2, nz, False, 0.5))
    return times_left(pairs(ny // 2, ny, True, 0.5), narrow)


def prolonged(coarse):
    cy, cz = coarse.shape
    right = pairs(cz, 2 * cz, True, 1.0)
    left = pairs(cy, 2 * cy, False, 1.0)
    dot = functools.partial(jnp.dot, preferred_element_type=F32)
    total = None
    for piece in pieces(coarse):
        wide = dot(left, dot(piece, right).astype(BF16))
        total = wide if total is None else total + wide
    return total


def looked_up(table_ref, classes):
    values = jnp.full(classes.shape, table_ref[0], F32)
    for entry in range(1, table_ref.shape[0]):
        values = jnp.where(classes == entry, table_ref[entry], values)
    return values


def coefficients(moments):
    def inner(a, b):
        total = None
        for i, x in enumerate(a):
            for j, y in enumerate(b):
                term = x * y * moments[i + j]
                total = term if total is None else total + term
        return total

    one = jnp.ones_like(moments[0])
    residual, direction, solution = [one], [one], []
    norm_now = moments[0]
    for step in range(ITERS):
        image = [CENTRE * d for d in direction] + [0.0 * one]
        for i, d in enumerate(direction):
            image[i + 1] = image[i + 1] - BESIDE * d
        alpha = norm_now / inner(direction, image)
        alpha = jnp.clip(alpha, 1.0 / HIGHEST, 1.0 / LOWEST)
        for i, d in enumerate(direction):
            if i < len(solution):
                solution[i] = solution[i] + alpha * d
            else:
                solution.append(alpha * d)
        if step == ITERS - 1:
            break
        residual = residual + [0.0 * one]
        residual = [r - alpha * a for r, a in zip(residual, image)]
        norm_next = inner(residual, residual)
        beta = jnp.clip(norm_next / norm_now, 0.0, HIGHEST - LOWEST)
        direction = [r + beta * d for r, d in zip(residual, direction + [0.0 * one])]
        norm_now = norm_next
    return solution


def kernel(S, T, state_ref, classes_ref, perm_hbm, rate_hbm, out_ref,
           ext, extk, cbuf, kbuf, nbuf, dbuf, w0, w1, w2, w3, d0, d1, d2, perm_buf,
           perm_ref, rate_ref, rs_buf, ratio_buf, msrc, mbuf, jsrc, jbuf, gsrc, gbuf, hsrc, hbuf, parts_of,
           local_sem, c_send, c_recv, k_send, k_recv, f_send, f_recv, m_send, m_recv,
           j_send, j_recv, g_send, g_recv, h_send, h_recv):
    NY, NZ = state_ref.shape
    rows = NY // S
    slab = rows + 2 * HALO
    own = slice(HALO, HALO + rows)
    me = lax.axis_index("space")
    t = lax.axis_index("tm")

    local = []
    for n, (source, target) in enumerate(((state_ref, ext), (classes_ref, extk))):
        local += [
            pltpu.make_async_copy(source, target.at[pl.ds(HALO, NY)], local_sem.at[3 * n]),
            pltpu.make_async_copy(
                source.at[pl.ds(NY - HALO, HALO)], target.at[pl.ds(0, HALO)], local_sem.at[3 * n + 1]),
            pltpu.make_async_copy(
                source.at[pl.ds(0, HALO)], target.at[pl.ds(HALO + NY, HALO)], local_sem.at[3 * n + 2]),
        ]
    local += [
        pltpu.make_async_copy(perm_hbm, perm_ref, local_sem.at[6]),
        pltpu.make_async_copy(rate_hbm, rate_ref, local_sem.at[7]),
    ]
    for copy in local:
        copy.start()

    barrier = pltpu.get_barrier_semaphore()
    partners = [(dt, dz) for dt in range(T) for dz in range(S) if dz == 0 or dt in (0, 1, T - 1)][1:]
    for dt, dz in partners:
        pl.semaphore_signal(
            barrier, inc=1,
            device_id={"tm": lax.rem(t + dt, T), "space": lax.rem(me + dz, S)},
            device_id_type=pl.DeviceIdType.MESH)
    for copy in local:
        copy.wait()
    pl.semaphore_wait(barrier, len(partners))

    high, wide = slab // 2, NZ // 2
    row_part, lane_part = lax.rem(t, 2), lax.div(t, 2)
    lanes = pl.ds(pl.multiple_of(lane_part * wide, 128), wide)
    quarter_rows = pl.ds(pl.multiple_of(row_part * high, 8), high)

    def class_copy(d):
        to = lax.rem(me + d, S)
        start = pl.multiple_of(to * rows + row_part * high, 8)
        return pltpu.make_async_remote_copy(
            src_ref=extk.at[pl.ds(start, high), lanes],
            dst_ref=kbuf.at[me, quarter_rows, lanes],
            send_sem=k_send.at[d - 1], recv_sem=k_recv.at[d - 1],
            device_id={"space": to}, device_id_type=pl.DeviceIdType.MESH)

    def class_forward(d, e):
        place = kbuf.at[lax.rem(me + S - d, S), quarter_rows, lanes]
        return pltpu.make_async_remote_copy(
            src_ref=place, dst_ref=place,
            send_sem=f_send.at[d - 1, e - 1], recv_sem=f_recv.at[d - 1, e - 1],
            device_id={"tm": lax.rem(t + e, T)}, device_id_type=pl.DeviceIdType.MESH)

    def slab_copy(d):
        to = lax.rem(me + d, S)
        return pltpu.make_async_remote_copy(
            src_ref=ext.at[pl.ds(pl.multiple_of(to * rows, 8), slab)],
            dst_ref=cbuf.at[me],
            send_sem=c_send.at[d - 1], recv_sem=c_recv.at[d - 1],
            device_id={"space": to}, device_id_type=pl.DeviceIdType.MESH)

    k_copies = [class_copy(d) for d in range(1, S)]
    c_copies = [slab_copy(d) for d in range(1, S)]
    f_copies = [class_forward(d, e) for d in range(1, S) for e in range(1, T)]
    for copy in k_copies:
        copy.start()
    for copy in c_copies:
        copy.start()
    mine = pl.ds(pl.multiple_of(me * rows, 8), slab)
    cbuf[me] = ext[mine]
    kbuf[me] = extk[mine]

    @pl.when(t == 0)
    def _():
        out_ref[...] = ext[HALO:HALO + NY]

    for d in range(1, S):
        k_copies[d - 1].wait_recv()
        for e in range(1, T):
            f_copies[(d - 1) * (T - 1) + e - 1].start()

    lane = lax.broadcasted_iota(jnp.int32, (slab, NZ), 1)

    def vertical_pair(value):
        upper = jnp.where(lane == NZ - 1, 0.0, pltpu.roll(value, NZ - 1, 1))
        lower = jnp.where(lane == 0, 0.0, pltpu.roll(value, 1, 1))
        return upper, lower

    def apart(value):
        upper, lower = vertical_pair(value)
        return upper - lower

    def neighbours(ref, p):
        value = ref[p]
        upper, lower = vertical_pair(value)
        total = (upper + lower) + (ref[(p + 1) % S] + ref[(p + S - 1) % S])
        total = total + (pltpu.roll(value, 1, 0) + pltpu.roll(value, slab - 1, 0))
        return SCALE * total

    def dot_rows(a, b):
        product = (a * b)[own]
        return product.reshape(rows // 8, 8, NZ).sum(axis=0)

    for copy in c_copies:
        copy.wait_recv()
    for p in range(S):
        nbuf[p] = neighbours(cbuf, p)
        dbuf[p] = apart(cbuf[p])
    for copy in f_copies:
        copy.wait_recv()
    for p in range(S):
        c = cbuf[p]
        perm = looked_up(perm_ref, kbuf[p])
        perm_buf[p] = perm
        w0[p] = c - ADV * perm * c * dbuf[p] - CENTRE * c + BESIDE * nbuf[p]

    def arriving(source, target, send, recv, p):
        return pltpu.make_async_remote_copy(
            src_ref=source, dst_ref=target, send_sem=send, recv_sem=recv,
            device_id={"tm": lax.rem(t + 1, T), "space": p}, device_id_type=pl.DeviceIdType.MESH)

    def jump_copy(p):
        return arriving(jsrc.at[p], jbuf.at[me], j_send.at[p], j_recv.at[me], p)

    def coarse_copy(p):
        return arriving(gsrc.at[p], gbuf.at[me], g_send.at[p], g_recv.at[me], p)

    def slab_send(source, slot, ahead, send):
        return pltpu.make_async_remote_copy(
            src_ref=source, dst_ref=hbuf.at[slot], send_sem=h_send.at[send], recv_sem=h_recv.at[slot],
            device_id={"tm": lax.rem(t + ahead, T)}, device_id_type=pl.DeviceIdType.MESH)

    near_copy = slab_send(hsrc, 0, 1, 0)
    far_copy = slab_send(hsrc, 0, 2, 1)
    next_copy = slab_send(hsrc, 1, 1, 0)
    start_copy = slab_send(rs_buf, 2, 1, 2)

    krylov = (w0, w1, w2, w3)
    for fine in range(FINE):
        sums = [None] * MOMENTS
        for k in range(ITERS):
            source, target = krylov[k], krylov[k + 1]
            for p in range(S):
                value = neighbours(source, p)
                target[p] = value
                here = source[p]
                for order, term in ((2 * k, dot_rows(here, here)), (2 * k + 1, dot_rows(here, value))):
                    sums[order] = term if sums[order] is None else sums[order] + term
        lines = [jnp.sum(s[:, :NZ // 2] + s[:, NZ // 2:], axis=0, keepdims=True) for s in sums]
        lines = lines + [jnp.zeros_like(lines[0])] * (8 - MOMENTS)
        msrc[fine] = jnp.concatenate(lines, axis=0)
        mbuf[fine, me] = msrc[fine]
        m_copies = [
            pltpu.make_async_remote_copy(
                src_ref=msrc.at[fine], dst_ref=mbuf.at[fine, me],
                send_sem=m_send.at[fine, d - 1], recv_sem=m_recv.at[fine, d - 1],
                device_id={"space": lax.rem(me + d, S)}, device_id_type=pl.DeviceIdType.MESH)
            for d in range(1, S)
        ]
        for copy in m_copies:
            copy.start()
        if fine < FINE - 1:
            for p in range(S):
                d0[p] = apart(w0[p])
                d1[p] = apart(w1[p])
                d2[p] = apart(w2[p])
        if fine == 0:
            whole = jnp.concatenate([cbuf[p][own] for p in range(S)], axis=0)
            kinds = jnp.concatenate([kbuf[p][own] for p in range(S)], axis=0)
            ratio_buf[...] = 1.0 / (1.0 + restricted(looked_up(rate_ref, kinds)))
            rs_buf[...] = restricted(whole)

            @pl.when(t == 1)
            def _():
                start_copy.start()
        if fine == FINE - 1:
            for n, ref in enumerate((cbuf, w0, w1, w2)):
                parts_of[n] = restricted(jnp.concatenate([ref[p][own] for p in range(S)], axis=0))
        for copy in m_copies:
            copy.wait()
        total = mbuf[fine, 0]
        for d in range(1, S):
            total = total + mbuf[fine, d]
        total = jnp.sum(total, axis=1, keepdims=True)
        found = [jnp.broadcast_to(total[k:k + 1, :], (1, NZ)) for k in range(MOMENTS)]
        a = coefficients(found)
        if fine < FINE - 1:
            for p in range(S):
                x0, x1, x2, x3 = w0[p], w1[p], w2[p], w3[p]
                c = cbuf[p] + a[0] * x0 + a[1] * x1 + a[2] * x2
                near = nbuf[p] + a[0] * x1 + a[1] * x2 + a[2] * x3
                apart_c = dbuf[p] + a[0] * d0[p] + a[1] * d1[p] + a[2] * d2[p]
                cbuf[p] = c
                nbuf[p] = near
                dbuf[p] = apart_c
                w0[p] = c - ADV * perm_buf[p] * c * apart_c - CENTRE * c + BESIDE * near
        else:
            half = [x[:, :NZ // 2] for x in a]
            hsrc[...] = parts_of[0] + (half[0] * parts_of[1] + half[1] * parts_of[2] + half[2] * parts_of[3])

            @pl.when(t == 0)
            def _():
                far_copy.start()
                near_copy.start()

            @pl.when(t == 1)
            def _():
                next_copy.start()

            for p in range(S):
                jsrc[p] = cbuf[p][own] + (a[0] * w0[p][own] + a[1] * w1[p][own] + a[2] * w2[p][own])

                @pl.when(t < T - 1)
                def _():
                    jump_copy(p).start()

    @pl.when(t == 1)
    def _():
        near_copy.wait_recv()
        gsrc[...] = (ratio_buf[...] * (hbuf[0] - rs_buf[...])).reshape(S, rows // 2, NZ // 2)

    @pl.when(t == 2)
    def _():
        start_copy.wait_recv()
        near_copy.wait_recv()
        first = ratio_buf[...] * (hbuf[0] - hbuf[2]) - rs_buf[...]
        next_copy.wait_recv()
        gsrc[...] = (ratio_buf[...] * (first + hbuf[1])).reshape(S, rows // 2, NZ // 2)

    @pl.when((t > 0) & (t < T - 1))
    def _():
        for p in range(S):
            coarse_copy(p).start()

    @pl.when(t > 1)
    def _():
        for p in range(S):
            arriving(gsrc.at[p], gbuf.at[p], g_send.at[p], g_recv.at[p], p).wait_recv()
        out_ref[...] = prolonged(gbuf[...].reshape(NY // 2, NZ // 2))

    @pl.when(t == 1)
    def _():
        out_ref[...] = jnp.zeros_like(out_ref)

    @pl.when(t > 0)
    def _():
        for p in range(S):
            arriving(jsrc.at[p], jbuf.at[p], j_send.at[p], j_recv.at[p], p).wait_recv()
        out_ref[...] += jbuf[...].reshape(NY, NZ)

    for copy in c_copies + k_copies + f_copies:
        copy.wait_send()

    @pl.when(t < T - 1)
    def _():
        for p in range(S):
            jump_copy(p).wait_send()

    @pl.when(t == 0)
    def _():
        far_copy.wait_send()
        near_copy.wait_send()

    @pl.when(t == 1)
    def _():
        next_copy.wait_send()
        start_copy.wait_send()

    @pl.when((t > 0) & (t < T - 1))
    def _():
        for p in range(S):
            coarse_copy(p).wait_send()


def fused_body(S, T, state, classes, perm_table, rate_table):
    ny, nz = state.shape[2:]
    rows = ny // S
    slab = rows + 2 * HALO
    field = pltpu.VMEM((S, slab, nz), F32)
    coarse = pltpu.VMEM((ny // 2, nz // 2), F32)
    dma = pltpu.SemaphoreType.DMA
    updated = pl.pallas_call(
        functools.partial(kernel, S, T),
        out_shape=jax.ShapeDtypeStruct((ny, nz), F32),
        in_specs=[pl.BlockSpec(memory_space=pltpu.HBM)] * 4,
        out_specs=pl.BlockSpec(memory_space=pltpu.VMEM),
        scratch_shapes=[
            pltpu.VMEM((ny + 2 * HALO, nz), F32),
            pltpu.VMEM((ny + 2 * HALO, nz), jnp.int32),
            field,
            pltpu.VMEM((S, slab, nz), jnp.int32),
        ] + [field] * 10 + [
            pltpu.SMEM(perm_table.shape, F32),
            pltpu.SMEM(rate_table.shape, F32),
            coarse,
            coarse,
            pltpu.VMEM((FINE, 8, nz // 2), F32),
            pltpu.VMEM((FINE, S, 8, nz // 2), F32),
            pltpu.VMEM((S, rows, nz), F32),
            pltpu.VMEM((S, rows, nz), F32),
            pltpu.VMEM((S, rows // 2, nz // 2), F32),
            pltpu.VMEM((S, rows // 2, nz // 2), F32),
            coarse,
            pltpu.VMEM((3, ny // 2, nz // 2), F32),
            pltpu.VMEM((4, ny // 2, nz // 2), F32),
            dma((8,)),
            dma((S - 1,)), dma((S - 1,)),
            dma((S - 1,)), dma((S - 1,)),
            dma((S - 1, T - 1)), dma((S - 1, T - 1)),
            dma((FINE, S - 1)), dma((FINE, S - 1)),
            dma((S,)), dma((S,)),
            dma((S,)), dma((S,)),
            dma((3,)), dma((3,)),
        ],
        compiler_params=pltpu.CompilerParams(
            collective_id=0, has_side_effects=True, vmem_limit_bytes=56 * 1024 * 1024),
    )(state[0, 0], classes[0], perm_table, rate_table)
    return updated[None, None]


def with_halo(array, sides, width):
    for axis, dim in sides:
        devices, length = (lax.axis_size(axis), array.shape[dim])
        up = [(i, (i + 1) % devices) for i in range(devices)]
        down = [(j, i) for i, j in up]
        last = lax.slice_in_dim(array, length - width, length, axis=dim)
        first = lax.slice_in_dim(array, 0, width, axis=dim)
        before = lax.ppermute(last, axis, up)
        after = lax.ppermute(first, axis, down)
        array = jnp.concatenate([before, array, after], axis=dim)
    return array


def passed_along(array, axis, by):
    devices = lax.axis_size(axis)
    pairs = [(i, i + by) for i in range(devices) if 0 <= i + by < devices]
    return lax.ppermute(array, axis, pairs)


def lookup(table, classes):
    values = jnp.zeros(classes.shape, jnp.float32)
    for entry in range(table.shape[0]):
        values = jnp.where(classes == entry, table[entry], values)
    return values


def restrict(field):
    cx, ny, nz = field.shape
    return field.reshape(cx, ny // 2, 2, nz // 2, 2).mean(axis=(2, 4))


def prolong(coarse):
    return jnp.repeat(jnp.repeat(coarse, 2, axis=1), 2, axis=2)


def vertical(field):
    zero_plane = jnp.zeros(field.shape[:2] + (1,), jnp.float32)
    upper = jnp.concatenate([field[:, :, 1:], zero_plane], axis=2)
    lower = jnp.concatenate([zero_plane, field[:, :, :-1]], axis=2)
    return (upper, lower)


def operate(field):
    padded = with_halo(field, (("space", 0),), 1)
    upper, lower = vertical(field)
    beside = padded[2:] + padded[:-2]
    beside = beside + jnp.roll(field, -1, 1) + jnp.roll(field, 1, 1)
    beside = beside + upper + lower
    return (1.0 + 6.0 * DIFF) * field - DIFF * beside


def squares(residual):
    return lax.psum(jnp.sum(residual * residual), "space")


def fine_step(field, perm):
    upper, lower = vertical(field)
    rhs = field - ADV * perm * field * (upper - lower)
    solution = field
    residual = rhs - operate(solution)
    direction = residual
    norm_now = squares(residual)
    for step in range(ITERS):
        image = operate(direction)
        alpha = norm_now / lax.psum(jnp.sum(direction * image), "space")
        solution = solution + alpha * direction
        residual = residual - alpha * image
        norm_next = squares(residual)
        direction = residual + norm_next / norm_now * direction
        norm_now = norm_next
    return solution


def body(state, classes, perm_table, rate_table):
    start = state[0]
    perm = lookup(perm_table, classes)
    coarse_ratio = 1.0 / (1.0 + restrict(lookup(rate_table, classes)))
    field = start
    for step in range(FINE):
        field = fine_step(field, perm)
    coarse_start = restrict(start)
    jump = field - prolong(coarse_ratio * coarse_start)
    jump_coarse = restrict(jump)
    first = lax.axis_index("tm") == 0
    factor = jnp.where(first, 0.0, coarse_ratio)
    offset = jnp.where(first, coarse_ratio * coarse_start + jump_coarse, jump_coarse)
    before = passed_along(jump, "tm", 1)
    before_coarse = restrict(before)

    def relay_turn(turn, carry):
        outgoing, received = carry
        received = passed_along(outgoing, "tm", 1)
        return (factor * received + offset, received)

    outgoing, received = lax.fori_loop(
        0, lax.axis_size("tm") - 1, relay_turn, (offset, jnp.zeros_like(offset))
    )
    updated = jnp.where(first, start, before + prolong(received - before_coarse))
    return updated[None]


def solution(mesh):
    placed = (
        P(("groups", "tm"), "space", None, None),
        P(("groups", "space"), None, None),
        P(),
        P(),
    )
    devices, slices = (mesh.shape["space"], mesh.shape["tm"])

    def chosen(state, classes, perm_table, rate_table):
        planes, ny, nz = state.shape[1:]
        fits = planes == 1 and ny // devices >= 4 * HALO and nz % 256 == 0
        if fits and slices == 4 and devices >= 3:
            return fused_body(devices, slices, state, classes, perm_table, rate_table)
        return body(state, classes, perm_table, rate_table)

    return jax.shard_map(
        chosen,
        mesh=mesh,
        in_specs=placed,
        out_specs=P(("groups", "tm"), "space", None, None),
        check_vma=False,
    )
```

```python
import functools

import jax
import jax.numpy as jnp
from jax import lax
from jax.experimental import pallas as pl
from jax.experimental.pallas import tpu as pltpu
from jax.sharding import PartitionSpec as P

ITERS = 3
FINE = 2


DIFF = 2.0
ADV = 0.25

CENTRE = 1.0 + 6.0 * DIFF
SCALE = 0.125
BESIDE = DIFF / SCALE
LOWEST = CENTRE - 6.0 * DIFF
HIGHEST = CENTRE + 6.0 * DIFF
HALO = 8
MOMENTS = 2 * ITERS
F32 = jnp.float32
BF16 = jnp.bfloat16


def pieces(value):
    high = value.astype(BF16)
    rest = value - high.astype(F32)
    middle = rest.astype(BF16)
    low = (rest - middle.astype(F32)).astype(BF16)
    return high, middle, low


def times(value, matrix):
    a, b, c = pieces(value)
    dot = functools.partial(jnp.dot, preferred_element_type=F32)
    return dot(a, matrix) + (dot(b, matrix) + dot(c, matrix))


def times_left(matrix, value):
    a, b, c = pieces(value)
    dot = functools.partial(jnp.dot, preferred_element_type=F32)
    return dot(matrix, a) + (dot(matrix, b) + dot(matrix, c))


def pairs(small, large, along, value):
    i = lax.broadcasted_iota(jnp.int32, (small, large) if along else (large, small), 0 if along else 1)
    j = lax.broadcasted_iota(jnp.int32, (small, large) if along else (large, small), 1 if along else 0)
    off = j - 2 * i
    return jnp.where((off == 0) | (off == 1), value, 0.0).astype(BF16)


def restricted(field):
    ny, nz = field.shape
    narrow = times(field, pairs(nz // 2, nz, False, 0.5))
    return times_left(pairs(ny // 2, ny, True, 0.5), narrow)


def prolonged(coarse):
    cy, cz = coarse.shape
    right = pairs(cz, 2 * cz, True, 1.0)
    left = pairs(cy, 2 * cy, False, 1.0)
    dot = functools.partial(jnp.dot, preferred_element_type=F32)
    total = None
    for piece in pieces(coarse):
        wide = dot(left, dot(piece, right).astype(BF16))
        total = wide if total is None else total + wide
    return total


def looked_up(table_ref, classes):
    values = jnp.full(classes.shape, table_ref[0], F32)
    for entry in range(1, table_ref.shape[0]):
        values = jnp.where(classes == entry, table_ref[entry], values)
    return values


def coefficients(moments):
    def inner(a, b):
        total = None
        for i, x in enumerate(a):
            for j, y in enumerate(b):
                term = x * y * moments[i + j]
                total = term if total is None else total + term
        return total

    one = jnp.ones_like(moments[0])
    residual, direction, solution = [one], [one], []
    norm_now = moments[0]
    for step in range(ITERS):
        image = [CENTRE * d for d in direction] + [0.0 * one]
        for i, d in enumerate(direction):
            image[i + 1] = image[i + 1] - BESIDE * d
        alpha = norm_now / inner(direction, image)
        alpha = jnp.clip(alpha, 1.0 / HIGHEST, 1.0 / LOWEST)
        for i, d in enumerate(direction):
            if i < len(solution):
                solution[i] = solution[i] + alpha * d
            else:
                solution.append(alpha * d)
        if step == ITERS - 1:
            break
        residual = residual + [0.0 * one]
        residual = [r - alpha * a for r, a in zip(residual, image)]
        norm_next = inner(residual, residual)
        beta = jnp.clip(norm_next / norm_now, 0.0, HIGHEST - LOWEST)
        direction = [r + beta * d for r, d in zip(residual, direction + [0.0 * one])]
        norm_now = norm_next
    return solution


def kernel(S, T, state_ref, classes_ref, perm_hbm, rate_hbm, out_ref,
           ext, extk, cbuf, kbuf, nbuf, dbuf, w0, w1, w2, w3, d0, d1, d2, perm_buf,
           perm_ref, rate_ref, rs_buf, ratio_buf, msrc, mbuf, jsrc, jbuf, gbuf, hsrc, sbuf, parts_of,
           local_sem, c_send, c_recv, k_send, k_recv, f_send, f_recv, m_send, m_recv,
           j_send, j_recv, g_send, g_recv, s_send, s_recv):
    NY, NZ = state_ref.shape
    rows = NY // S
    slab = rows + 2 * HALO
    own = slice(HALO, HALO + rows)
    me = lax.axis_index("space")
    t = lax.axis_index("tm")

    local = []
    for n, (source, target) in enumerate(((state_ref, ext), (classes_ref, extk))):
        local += [
            pltpu.make_async_copy(source, target.at[pl.ds(HALO, NY)], local_sem.at[3 * n]),
            pltpu.make_async_copy(
                source.at[pl.ds(NY - HALO, HALO)], target.at[pl.ds(0, HALO)], local_sem.at[3 * n + 1]),
            pltpu.make_async_copy(
                source.at[pl.ds(0, HALO)], target.at[pl.ds(HALO + NY, HALO)], local_sem.at[3 * n + 2]),
        ]
    local += [
        pltpu.make_async_copy(perm_hbm, perm_ref, local_sem.at[6]),
        pltpu.make_async_copy(rate_hbm, rate_ref, local_sem.at[7]),
    ]
    for copy in local:
        copy.start()

    barrier = pltpu.get_barrier_semaphore()
    partners = [(dt, dz) for dt in range(T) for dz in range(S)][1:]
    for dt, dz in partners:
        pl.semaphore_signal(
            barrier, inc=1,
            device_id={"tm": lax.rem(t + dt, T), "space": lax.rem(me + dz, S)},
            device_id_type=pl.DeviceIdType.MESH)
    for copy in local:
        copy.wait()
    pl.semaphore_wait(barrier, len(partners))

    high, wide = slab // 2, NZ // 2
    row_part, lane_part = lax.rem(t, 2), lax.div(t, 2)
    lanes = pl.ds(pl.multiple_of(lane_part * wide, 128), wide)
    quarter_rows = pl.ds(pl.multiple_of(row_part * high, 8), high)

    def class_copy(d):
        to = lax.rem(me + d, S)
        start = pl.multiple_of(to * rows + row_part * high, 8)
        return pltpu.make_async_remote_copy(
            src_ref=extk.at[pl.ds(start, high), lanes],
            dst_ref=kbuf.at[me, quarter_rows, lanes],
            send_sem=k_send.at[d - 1], recv_sem=k_recv.at[d - 1],
            device_id={"space": to}, device_id_type=pl.DeviceIdType.MESH)

    def class_forward(d, e):
        place = kbuf.at[lax.rem(me + S - d, S), quarter_rows, lanes]
        return pltpu.make_async_remote_copy(
            src_ref=place, dst_ref=place,
            send_sem=f_send.at[d - 1, e - 1], recv_sem=f_recv.at[d - 1, e - 1],
            device_id={"tm": lax.rem(t + e, T)}, device_id_type=pl.DeviceIdType.MESH)

    def slab_copy(d):
        to = lax.rem(me + d, S)
        return pltpu.make_async_remote_copy(
            src_ref=ext.at[pl.ds(pl.multiple_of(to * rows, 8), slab)],
            dst_ref=cbuf.at[me],
            send_sem=c_send.at[d - 1], recv_sem=c_recv.at[d - 1],
            device_id={"space": to}, device_id_type=pl.DeviceIdType.MESH)

    k_copies = [class_copy(d) for d in range(1, S)]
    c_copies = [slab_copy(d) for d in range(1, S)]
    f_copies = [class_forward(d, e) for d in range(1, S) for e in range(1, T)]
    for copy in k_copies:
        copy.start()
    for copy in c_copies:
        copy.start()
    mine = pl.ds(pl.multiple_of(me * rows, 8), slab)
    cbuf[me] = ext[mine]
    kbuf[me] = extk[mine]

    def start_send(slot, ahead):
        return pltpu.make_async_remote_copy(
            src_ref=rs_buf, dst_ref=sbuf.at[slot], send_sem=s_send.at[ahead - 1], recv_sem=s_recv.at[slot],
            device_id={"tm": lax.rem(t + ahead, T)}, device_id_type=pl.DeviceIdType.MESH)

    first_near, first_far, second_near = start_send(0, 1), start_send(0, 2), start_send(1, 1)
    rs_buf[...] = restricted(ext[HALO:HALO + NY])

    @pl.when(t == 0)
    def _():
        out_ref[...] = ext[HALO:HALO + NY]

    @pl.when(t == 1)
    def _():
        first_near.start()
        first_far.start()

    @pl.when(t == 2)
    def _():
        second_near.start()

    for d in range(1, S):
        k_copies[d - 1].wait_recv()
        for e in range(1, T):
            f_copies[(d - 1) * (T - 1) + e - 1].start()

    lane = lax.broadcasted_iota(jnp.int32, (slab, NZ), 1)

    def vertical_pair(value):
        upper = jnp.where(lane == NZ - 1, 0.0, pltpu.roll(value, NZ - 1, 1))
        lower = jnp.where(lane == 0, 0.0, pltpu.roll(value, 1, 1))
        return upper, lower

    def apart(value):
        upper, lower = vertical_pair(value)
        return upper - lower

    def neighbours(ref, p):
        value = ref[p]
        upper, lower = vertical_pair(value)
        total = (upper + lower) + (ref[(p + 1) % S] + ref[(p + S - 1) % S])
        total = total + (pltpu.roll(value, 1, 0) + pltpu.roll(value, slab - 1, 0))
        return SCALE * total

    def dot_rows(a, b):
        product = (a * b)[own]
        return product.reshape(rows // 8, 8, NZ).sum(axis=0)

    for copy in c_copies:
        copy.wait_recv()
    for p in range(S):
        nbuf[p] = neighbours(cbuf, p)
        dbuf[p] = apart(cbuf[p])
    for copy in f_copies:
        copy.wait_recv()
    for p in range(S):
        c = cbuf[p]
        perm = looked_up(perm_ref, kbuf[p])
        perm_buf[p] = perm
        w0[p] = c - ADV * perm * c * dbuf[p] - CENTRE * c + BESIDE * nbuf[p]

    def arriving(source, target, send, recv, p):
        return pltpu.make_async_remote_copy(
            src_ref=source, dst_ref=target, send_sem=send, recv_sem=recv,
            device_id={"tm": lax.rem(t + 1, T), "space": p}, device_id_type=pl.DeviceIdType.MESH)

    def jump_copy(p):
        return arriving(jsrc.at[p], jbuf.at[me], j_send.at[p], j_recv.at[me], p)

    def coarse_copy(p, slot, ahead):
        return pltpu.make_async_remote_copy(
            src_ref=hsrc.at[p], dst_ref=gbuf.at[slot, me],
            send_sem=g_send.at[ahead - 2, p], recv_sem=g_recv.at[slot, me],
            device_id={"tm": lax.rem(t + ahead, T), "space": p}, device_id_type=pl.DeviceIdType.MESH)

    krylov = (w0, w1, w2, w3)
    for fine in range(FINE):
        sums = [None] * MOMENTS
        for k in range(ITERS):
            source, target = krylov[k], krylov[k + 1]
            for p in range(S):
                value = neighbours(source, p)
                target[p] = value
                here = source[p]
                for order, term in ((2 * k, dot_rows(here, here)), (2 * k + 1, dot_rows(here, value))):
                    sums[order] = term if sums[order] is None else sums[order] + term
        lines = [jnp.sum(s[:, :NZ // 2] + s[:, NZ // 2:], axis=0, keepdims=True) for s in sums]
        lines = lines + [jnp.zeros_like(lines[0])] * (8 - MOMENTS)
        msrc[fine] = jnp.concatenate(lines, axis=0)
        mbuf[fine, me] = msrc[fine]
        m_copies = [
            pltpu.make_async_remote_copy(
                src_ref=msrc.at[fine], dst_ref=mbuf.at[fine, me],
                send_sem=m_send.at[fine, d - 1], recv_sem=m_recv.at[fine, d - 1],
                device_id={"space": lax.rem(me + d, S)}, device_id_type=pl.DeviceIdType.MESH)
            for d in range(1, S)
        ]
        for copy in m_copies:
            copy.start()
        if fine < FINE - 1:
            for p in range(S):
                d0[p] = apart(w0[p])
                d1[p] = apart(w1[p])
                d2[p] = apart(w2[p])
        if fine == 0:
            ratio_buf[...] = 1.0 / (1.0 + restricted(looked_up(rate_ref, extk[HALO:HALO + NY])))
        if fine == FINE - 1:
            for n, ref in enumerate((cbuf, w0, w1, w2)):
                parts_of[n] = restricted(jnp.concatenate([ref[p][own] for p in range(S)], axis=0))
        for copy in m_copies:
            copy.wait()
        total = mbuf[fine, 0]
        for d in range(1, S):
            total = total + mbuf[fine, d]
        total = jnp.sum(total, axis=1, keepdims=True)
        found = [jnp.broadcast_to(total[k:k + 1, :], (1, NZ)) for k in range(MOMENTS)]
        a = coefficients(found)
        if fine < FINE - 1:
            for p in range(S):
                x0, x1, x2, x3 = w0[p], w1[p], w2[p], w3[p]
                c = cbuf[p] + a[0] * x0 + a[1] * x1 + a[2] * x2
                near = nbuf[p] + a[0] * x1 + a[1] * x2 + a[2] * x3
                apart_c = dbuf[p] + a[0] * d0[p] + a[1] * d1[p] + a[2] * d2[p]
                cbuf[p] = c
                nbuf[p] = near
                dbuf[p] = apart_c
                w0[p] = c - ADV * perm_buf[p] * c * apart_c - CENTRE * c + BESIDE * near
        else:
            half = [x[:, :NZ // 2] for x in a]
            ends = parts_of[0] + (half[0] * parts_of[1] + half[1] * parts_of[2] + half[2] * parts_of[3])
            hsrc[...] = ends.reshape(S, rows // 2, NZ // 2)

            @pl.when(t == 0)
            def _():
                for p in range(S):
                    coarse_copy(p, 0, 3).start()
                    coarse_copy(p, 0, 2).start()

            @pl.when(t == 1)
            def _():
                for p in range(S):
                    coarse_copy(p, 1, 2).start()

            for p in range(S):
                jsrc[p] = cbuf[p][own] + (a[0] * w0[p][own] + a[1] * w1[p][own] + a[2] * w2[p][own])

                @pl.when(t < T - 1)
                def _():
                    jump_copy(p).start()

    def coarse_end(slot):
        for p in range(S):
            arriving(hsrc.at[p], gbuf.at[slot, p], g_send.at[0, p], g_recv.at[slot, p], p).wait_recv()
        return gbuf[slot].reshape(NY // 2, NZ // 2)

    @pl.when(t == 2)
    def _():
        first_near.wait_recv()
        out_ref[...] = prolonged(ratio_buf[...] * (coarse_end(0) - sbuf[0]))

    @pl.when(t == 3)
    def _():
        first_near.wait_recv()
        second_near.wait_recv()
        ratio = ratio_buf[...]
        second = ratio * (coarse_end(0) - sbuf[0]) + (coarse_end(1) - sbuf[1])
        out_ref[...] = prolonged(ratio * second)

    @pl.when(t == 1)
    def _():
        out_ref[...] = jnp.zeros_like(out_ref)

    @pl.when(t > 0)
    def _():
        for p in range(S):
            arriving(jsrc.at[p], jbuf.at[p], j_send.at[p], j_recv.at[p], p).wait_recv()
        out_ref[...] += jbuf[...].reshape(NY, NZ)

    for copy in c_copies + k_copies + f_copies:
        copy.wait_send()

    @pl.when(t < T - 1)
    def _():
        for p in range(S):
            jump_copy(p).wait_send()

    @pl.when(t == 0)
    def _():
        for p in range(S):
            coarse_copy(p, 0, 3).wait_send()
            coarse_copy(p, 0, 2).wait_send()

    @pl.when(t == 1)
    def _():
        first_near.wait_send()
        first_far.wait_send()
        for p in range(S):
            coarse_copy(p, 1, 2).wait_send()

    @pl.when(t == 2)
    def _():
        second_near.wait_send()


def fused_body(S, T, state, classes, perm_table, rate_table):
    ny, nz = state.shape[2:]
    rows = ny // S
    slab = rows + 2 * HALO
    field = pltpu.VMEM((S, slab, nz), F32)
    coarse = pltpu.VMEM((ny // 2, nz // 2), F32)
    dma = pltpu.SemaphoreType.DMA
    updated = pl.pallas_call(
        functools.partial(kernel, S, T),
        out_shape=jax.ShapeDtypeStruct((ny, nz), F32),
        in_specs=[pl.BlockSpec(memory_space=pltpu.HBM)] * 4,
        out_specs=pl.BlockSpec(memory_space=pltpu.VMEM),
        scratch_shapes=[
            pltpu.VMEM((ny + 2 * HALO, nz), F32),
            pltpu.VMEM((ny + 2 * HALO, nz), jnp.int32),
            field,
            pltpu.VMEM((S, slab, nz), jnp.int32),
        ] + [field] * 10 + [
            pltpu.SMEM(perm_table.shape, F32),
            pltpu.SMEM(rate_table.shape, F32),
            coarse,
            coarse,
            pltpu.VMEM((FINE, 8, nz // 2), F32),
            pltpu.VMEM((FINE, S, 8, nz // 2), F32),
            pltpu.VMEM((S, rows, nz), F32),
            pltpu.VMEM((S, rows, nz), F32),
            pltpu.VMEM((2, S, rows // 2, nz // 2), F32),
            pltpu.VMEM((S, rows // 2, nz // 2), F32),
            pltpu.VMEM((2, ny // 2, nz // 2), F32),
            pltpu.VMEM((4, ny // 2, nz // 2), F32),
            dma((8,)),
            dma((S - 1,)), dma((S - 1,)),
            dma((S - 1,)), dma((S - 1,)),
            dma((S - 1, T - 1)), dma((S - 1, T - 1)),
            dma((FINE, S - 1)), dma((FINE, S - 1)),
            dma((S,)), dma((S,)),
            dma((2, S)), dma((2, S)),
            dma((2,)), dma((2,)),
        ],
        compiler_params=pltpu.CompilerParams(
            collective_id=0, has_side_effects=True, vmem_limit_bytes=56 * 1024 * 1024),
    )(state[0, 0], classes[0], perm_table, rate_table)
    return updated[None, None]


def with_halo(array, sides, width):
    for axis, dim in sides:
        devices, length = (lax.axis_size(axis), array.shape[dim])
        up = [(i, (i + 1) % devices) for i in range(devices)]
        down = [(j, i) for i, j in up]
        last = lax.slice_in_dim(array, length - width, length, axis=dim)
        first = lax.slice_in_dim(array, 0, width, axis=dim)
        before = lax.ppermute(last, axis, up)
        after = lax.ppermute(first, axis, down)
        array = jnp.concatenate([before, array, after], axis=dim)
    return array


def passed_along(array, axis, by):
    devices = lax.axis_size(axis)
    pairs = [(i, i + by) for i in range(devices) if 0 <= i + by < devices]
    return lax.ppermute(array, axis, pairs)


def lookup(table, classes):
    values = jnp.zeros(classes.shape, jnp.float32)
    for entry in range(table.shape[0]):
        values = jnp.where(classes == entry, table[entry], values)
    return values


def restrict(field):
    cx, ny, nz = field.shape
    return field.reshape(cx, ny // 2, 2, nz // 2, 2).mean(axis=(2, 4))


def prolong(coarse):
    return jnp.repeat(jnp.repeat(coarse, 2, axis=1), 2, axis=2)


def vertical(field):
    zero_plane = jnp.zeros(field.shape[:2] + (1,), jnp.float32)
    upper = jnp.concatenate([field[:, :, 1:], zero_plane], axis=2)
    lower = jnp.concatenate([zero_plane, field[:, :, :-1]], axis=2)
    return (upper, lower)


def operate(field):
    padded = with_halo(field, (("space", 0),), 1)
    upper, lower = vertical(field)
    beside = padded[2:] + padded[:-2]
    beside = beside + jnp.roll(field, -1, 1) + jnp.roll(field, 1, 1)
    beside = beside + upper + lower
    return (1.0 + 6.0 * DIFF) * field - DIFF * beside


def squares(residual):
    return lax.psum(jnp.sum(residual * residual), "space")


def fine_step(field, perm):
    upper, lower = vertical(field)
    rhs = field - ADV * perm * field * (upper - lower)
    solution = field
    residual = rhs - operate(solution)
    direction = residual
    norm_now = squares(residual)
    for step in range(ITERS):
        image = operate(direction)
        alpha = norm_now / lax.psum(jnp.sum(direction * image), "space")
        solution = solution + alpha * direction
        residual = residual - alpha * image
        norm_next = squares(residual)
        direction = residual + norm_next / norm_now * direction
        norm_now = norm_next
    return solution


def body(state, classes, perm_table, rate_table):
    start = state[0]
    perm = lookup(perm_table, classes)
    coarse_ratio = 1.0 / (1.0 + restrict(lookup(rate_table, classes)))
    field = start
    for step in range(FINE):
        field = fine_step(field, perm)
    coarse_start = restrict(start)
    jump = field - prolong(coarse_ratio * coarse_start)
    jump_coarse = restrict(jump)
    first = lax.axis_index("tm") == 0
    factor = jnp.where(first, 0.0, coarse_ratio)
    offset = jnp.where(first, coarse_ratio * coarse_start + jump_coarse, jump_coarse)
    before = passed_along(jump, "tm", 1)
    before_coarse = restrict(before)

    def relay_turn(turn, carry):
        outgoing, received = carry
        received = passed_along(outgoing, "tm", 1)
        return (factor * received + offset, received)

    outgoing, received = lax.fori_loop(
        0, lax.axis_size("tm") - 1, relay_turn, (offset, jnp.zeros_like(offset))
    )
    updated = jnp.where(first, start, before + prolong(received - before_coarse))
    return updated[None]


def solution(mesh):
    placed = (
        P(("groups", "tm"), "space", None, None),
        P(("groups", "space"), None, None),
        P(),
        P(),
    )
    devices, slices = (mesh.shape["space"], mesh.shape["tm"])

    def chosen(state, classes, perm_table, rate_table):
        planes, ny, nz = state.shape[1:]
        fits = planes == 1 and ny // devices >= 4 * HALO and nz % 256 == 0
        if fits and slices == 4 and devices >= 3:
            return fused_body(devices, slices, state, classes, perm_table, rate_table)
        return body(state, classes, perm_table, rate_table)

    return jax.shard_map(
        chosen,
        mesh=mesh,
        in_specs=placed,
        out_specs=P(("groups", "tm"), "space", None, None),
        check_vma=False,
    )
```

```python
import functools

import jax
import jax.numpy as jnp
from jax import lax
from jax.experimental import pallas as pl
from jax.experimental.pallas import tpu as pltpu
from jax.sharding import PartitionSpec as P

ITERS = 3
FINE = 2


DIFF = 2.0
ADV = 0.25

CENTRE = 1.0 + 6.0 * DIFF
BESIDE = DIFF
LOWEST = CENTRE - 6.0 * DIFF
HIGHEST = CENTRE + 6.0 * DIFF
HALO = 8
MOMENTS = 2 * ITERS
F32 = jnp.float32
BF16 = jnp.bfloat16


def pieces(value):
    high = value.astype(BF16)
    rest = value - high.astype(F32)
    middle = rest.astype(BF16)
    low = (rest - middle.astype(F32)).astype(BF16)
    return high, middle, low


def times(value, matrix):
    a, b, c = pieces(value)
    dot = functools.partial(jnp.dot, preferred_element_type=F32)
    return dot(a, matrix) + (dot(b, matrix) + dot(c, matrix))


def times_left(matrix, value):
    a, b, c = pieces(value)
    dot = functools.partial(jnp.dot, preferred_element_type=F32)
    return dot(matrix, a) + (dot(matrix, b) + dot(matrix, c))


def pairs(small, large, along, value):
    i = lax.broadcasted_iota(jnp.int32, (small, large) if along else (large, small), 0 if along else 1)
    j = lax.broadcasted_iota(jnp.int32, (small, large) if along else (large, small), 1 if along else 0)
    off = j - 2 * i
    return jnp.where((off == 0) | (off == 1), value, 0.0).astype(BF16)


def restricted(field):
    ny, nz = field.shape
    narrow = times(field, pairs(nz // 2, nz, False, 0.5))
    return times_left(pairs(ny // 2, ny, True, 0.5), narrow)


def prolonged(coarse):
    cy, cz = coarse.shape
    right = pairs(cz, 2 * cz, True, 1.0)
    left = pairs(cy, 2 * cy, False, 1.0)
    dot = functools.partial(jnp.dot, preferred_element_type=F32)
    total = None
    for piece in pieces(coarse):
        wide = dot(left, dot(piece, right).astype(BF16))
        total = wide if total is None else total + wide
    return total


def looked_up(table_ref, classes):
    values = jnp.full(classes.shape, table_ref[0], F32)
    for entry in range(1, table_ref.shape[0]):
        values = jnp.where(classes == entry, table_ref[entry], values)
    return values


def coefficients(moments):
    def inner(a, b):
        total = None
        for i, x in enumerate(a):
            for j, y in enumerate(b):
                term = x * y * moments[i + j]
                total = term if total is None else total + term
        return total

    one = jnp.ones_like(moments[0])
    residual, direction, solution = [one], [one], []
    norm_now = moments[0]
    for step in range(ITERS):
        image = [CENTRE * d for d in direction] + [0.0 * one]
        for i, d in enumerate(direction):
            image[i + 1] = image[i + 1] - BESIDE * d
        alpha = norm_now / inner(direction, image)
        alpha = jnp.clip(alpha, 1.0 / HIGHEST, 1.0 / LOWEST)
        for i, d in enumerate(direction):
            if i < len(solution):
                solution[i] = solution[i] + alpha * d
            else:
                solution.append(alpha * d)
        if step == ITERS - 1:
            break
        residual = residual + [0.0 * one]
        residual = [r - alpha * a for r, a in zip(residual, image)]
        norm_next = inner(residual, residual)
        beta = jnp.clip(norm_next / norm_now, 0.0, HIGHEST - LOWEST)
        direction = [r + beta * d for r, d in zip(residual, direction + [0.0 * one])]
        norm_now = norm_next
    return solution


def kernel(S, T, state_ref, classes_ref, perm_hbm, rate_hbm, out_ref,
           ext, extk, cbuf, kbuf, nbuf, dbuf, w0, w1, w2, w3, d0, d1, d2, perm_buf,
           perm_ref, rate_ref, rs_buf, ratio_buf, msrc, mbuf, jsrc, jbuf, gbuf, hsrc, sbuf, parts_of,
           local_sem, c_send, c_recv, k_send, k_recv, f_send, f_recv, m_send, m_recv,
           j_send, j_recv, g_send, g_recv, s_send, s_recv):
    NY, NZ = state_ref.shape
    rows = NY // S
    slab = rows + 2 * HALO
    own = slice(HALO, HALO + rows)
    me = lax.axis_index("space")
    t = lax.axis_index("tm")

    local = []
    for n, (source, target) in enumerate(((state_ref, ext), (classes_ref, extk))):
        local += [
            pltpu.make_async_copy(source, target.at[pl.ds(HALO, NY)], local_sem.at[3 * n]),
            pltpu.make_async_copy(
                source.at[pl.ds(NY - HALO, HALO)], target.at[pl.ds(0, HALO)], local_sem.at[3 * n + 1]),
            pltpu.make_async_copy(
                source.at[pl.ds(0, HALO)], target.at[pl.ds(HALO + NY, HALO)], local_sem.at[3 * n + 2]),
        ]
    local += [
        pltpu.make_async_copy(perm_hbm, perm_ref, local_sem.at[6]),
        pltpu.make_async_copy(rate_hbm, rate_ref, local_sem.at[7]),
    ]
    for copy in local:
        copy.start()

    barrier = pltpu.get_barrier_semaphore()
    partners = [(dt, dz) for dt in range(T) for dz in range(S)][1:]
    for dt, dz in partners:
        pl.semaphore_signal(
            barrier, inc=1,
            device_id={"tm": lax.rem(t + dt, T), "space": lax.rem(me + dz, S)},
            device_id_type=pl.DeviceIdType.MESH)
    for copy in local:
        copy.wait()
    pl.semaphore_wait(barrier, len(partners))

    high, wide = slab // 2, NZ // 2
    row_part, lane_part = lax.rem(t, 2), lax.div(t, 2)
    lanes = pl.ds(pl.multiple_of(lane_part * wide, 128), wide)
    quarter_rows = pl.ds(pl.multiple_of(row_part * high, 8), high)

    def class_copy(d):
        to = lax.rem(me + d, S)
        start = pl.multiple_of(to * rows + row_part * high, 8)
        return pltpu.make_async_remote_copy(
            src_ref=extk.at[pl.ds(start, high), lanes],
            dst_ref=kbuf.at[me, quarter_rows, lanes],
            send_sem=k_send.at[d - 1], recv_sem=k_recv.at[d - 1],
            device_id={"space": to}, device_id_type=pl.DeviceIdType.MESH)

    def class_forward(d, e):
        place = kbuf.at[lax.rem(me + S - d, S), quarter_rows, lanes]
        return pltpu.make_async_remote_copy(
            src_ref=place, dst_ref=place,
            send_sem=f_send.at[d - 1, e - 1], recv_sem=f_recv.at[d - 1, e - 1],
            device_id={"tm": lax.rem(t + e, T)}, device_id_type=pl.DeviceIdType.MESH)

    def slab_copy(d):
        to = lax.rem(me + d, S)
        return pltpu.make_async_remote_copy(
            src_ref=ext.at[pl.ds(pl.multiple_of(to * rows, 8), slab)],
            dst_ref=cbuf.at[me],
            send_sem=c_send.at[d - 1], recv_sem=c_recv.at[d - 1],
            device_id={"space": to}, device_id_type=pl.DeviceIdType.MESH)

    k_copies = [class_copy(d) for d in range(1, S)]
    c_copies = [slab_copy(d) for d in range(1, S)]
    f_copies = [class_forward(d, e) for d in range(1, S) for e in range(1, T)]
    for copy in k_copies:
        copy.start()
    for copy in c_copies:
        copy.start()
    mine = pl.ds(pl.multiple_of(me * rows, 8), slab)
    cbuf[me] = ext[mine]
    kbuf[me] = extk[mine]

    def start_send(slot, ahead):
        return pltpu.make_async_remote_copy(
            src_ref=rs_buf, dst_ref=sbuf.at[slot], send_sem=s_send.at[ahead - 1], recv_sem=s_recv.at[slot],
            device_id={"tm": lax.rem(t + ahead, T)}, device_id_type=pl.DeviceIdType.MESH)

    first_near, first_far, second_near = start_send(0, 1), start_send(0, 2), start_send(1, 1)
    rs_buf[...] = restricted(ext[HALO:HALO + NY])

    @pl.when(t == 0)
    def _():
        out_ref[...] = ext[HALO:HALO + NY]

    @pl.when(t == 1)
    def _():
        first_near.start()
        first_far.start()

    @pl.when(t == 2)
    def _():
        second_near.start()

    for d in range(1, S):
        k_copies[d - 1].wait_recv()
        for e in range(1, T):
            f_copies[(d - 1) * (T - 1) + e - 1].start()

    lane = lax.broadcasted_iota(jnp.int32, (slab, wide), 1)

    def vertical_pair(value):
        low, top = value[:, :wide], value[:, wide:]
        low_up, top_up = pltpu.roll(low, wide - 1, 1), pltpu.roll(top, wide - 1, 1)
        low_down, top_down = pltpu.roll(low, 1, 1), pltpu.roll(top, 1, 1)
        last, first = lane == wide - 1, lane == 0
        upper = (jnp.where(last, top_up, low_up), jnp.where(last, 0.0, top_up))
        lower = (jnp.where(first, 0.0, low_down), jnp.where(first, low_down, top_down))
        return jnp.concatenate(upper, axis=1), jnp.concatenate(lower, axis=1)

    def apart(value):
        upper, lower = vertical_pair(value)
        return upper - lower

    def neighbours(ref, p):
        value = ref[p]
        upper, lower = vertical_pair(value)
        total = (upper + lower) + (ref[(p + 1) % S] + ref[(p + S - 1) % S])
        total = total + (pltpu.roll(value, 1, 0) + pltpu.roll(value, slab - 1, 0))
        return total

    def dot_rows(a, b):
        product = (a * b)[own]
        return product.reshape(rows // 8, 8, NZ).sum(axis=0)

    for copy in c_copies:
        copy.wait_recv()
    for p in range(S):
        nbuf[p] = neighbours(cbuf, p)
        dbuf[p] = apart(cbuf[p])
    for copy in f_copies:
        copy.wait_recv()
    for p in range(S):
        c = cbuf[p]
        perm = looked_up(perm_ref, kbuf[p])
        perm_buf[p] = perm
        w0[p] = c - ADV * perm * c * dbuf[p] - CENTRE * c + BESIDE * nbuf[p]

    def arriving(source, target, send, recv, p):
        return pltpu.make_async_remote_copy(
            src_ref=source, dst_ref=target, send_sem=send, recv_sem=recv,
            device_id={"tm": lax.rem(t + 1, T), "space": p}, device_id_type=pl.DeviceIdType.MESH)

    def jump_copy(p):
        return arriving(jsrc.at[p], jbuf.at[me], j_send.at[p], j_recv.at[me], p)

    def coarse_copy(p, slot, ahead):
        return pltpu.make_async_remote_copy(
            src_ref=hsrc.at[p], dst_ref=gbuf.at[slot, me],
            send_sem=g_send.at[ahead - 2, p], recv_sem=g_recv.at[slot, me],
            device_id={"tm": lax.rem(t + ahead, T), "space": p}, device_id_type=pl.DeviceIdType.MESH)

    krylov = (w0, w1, w2, w3)
    for fine in range(FINE):
        sums = [None] * MOMENTS
        for k in range(ITERS):
            source, target = krylov[k], krylov[k + 1]
            for p in range(S):
                value = neighbours(source, p)
                target[p] = value
                here = source[p]
                for order, term in ((2 * k, dot_rows(here, here)), (2 * k + 1, dot_rows(here, value))):
                    sums[order] = term if sums[order] is None else sums[order] + term
        lines = [jnp.sum(s[:, :NZ // 2] + s[:, NZ // 2:], axis=0, keepdims=True) for s in sums]
        lines = lines + [jnp.zeros_like(lines[0])] * (8 - MOMENTS)
        msrc[fine] = jnp.concatenate(lines, axis=0)
        mbuf[fine, me] = msrc[fine]
        m_copies = [
            pltpu.make_async_remote_copy(
                src_ref=msrc.at[fine], dst_ref=mbuf.at[fine, me],
                send_sem=m_send.at[fine, d - 1], recv_sem=m_recv.at[fine, d - 1],
                device_id={"space": lax.rem(me + d, S)}, device_id_type=pl.DeviceIdType.MESH)
            for d in range(1, S)
        ]
        for copy in m_copies:
            copy.start()
        if fine < FINE - 1:
            for p in range(S):
                d0[p] = apart(w0[p])
                d1[p] = apart(w1[p])
                d2[p] = apart(w2[p])
        if fine == 0:
            ratio_buf[...] = 1.0 / (1.0 + restricted(looked_up(rate_ref, extk[HALO:HALO + NY])))
        if fine == FINE - 1:
            for n, ref in enumerate((cbuf, w0, w1, w2)):
                parts_of[n] = restricted(jnp.concatenate([ref[p][own] for p in range(S)], axis=0))
        for copy in m_copies:
            copy.wait()
        total = mbuf[fine, 0]
        for d in range(1, S):
            total = total + mbuf[fine, d]
        total = jnp.sum(total, axis=1, keepdims=True)
        found = [jnp.broadcast_to(total[k:k + 1, :], (1, NZ)) for k in range(MOMENTS)]
        a = coefficients(found)
        if fine < FINE - 1:
            for p in range(S):
                x0, x1, x2, x3 = w0[p], w1[p], w2[p], w3[p]
                c = cbuf[p] + a[0] * x0 + a[1] * x1 + a[2] * x2
                near = nbuf[p] + a[0] * x1 + a[1] * x2 + a[2] * x3
                apart_c = dbuf[p] + a[0] * d0[p] + a[1] * d1[p] + a[2] * d2[p]
                cbuf[p] = c
                nbuf[p] = near
                dbuf[p] = apart_c
                w0[p] = c - ADV * perm_buf[p] * c * apart_c - CENTRE * c + BESIDE * near
        else:
            half = [x[:, :NZ // 2] for x in a]
            ends = parts_of[0] + (half[0] * parts_of[1] + half[1] * parts_of[2] + half[2] * parts_of[3])
            hsrc[...] = ends.reshape(S, rows // 2, NZ // 2)

            @pl.when(t == 0)
            def _():
                for p in range(S):
                    coarse_copy(p, 0, 3).start()
                    coarse_copy(p, 0, 2).start()

            @pl.when(t == 1)
            def _():
                for p in range(S):
                    coarse_copy(p, 1, 2).start()

            for p in range(S):
                jsrc[p] = cbuf[p][own] + (a[0] * w0[p][own] + a[1] * w1[p][own] + a[2] * w2[p][own])

                @pl.when(t < T - 1)
                def _():
                    jump_copy(p).start()

    def coarse_end(slot):
        for p in range(S):
            arriving(hsrc.at[p], gbuf.at[slot, p], g_send.at[0, p], g_recv.at[slot, p], p).wait_recv()
        return gbuf[slot].reshape(NY // 2, NZ // 2)

    @pl.when(t == 2)
    def _():
        first_near.wait_recv()
        out_ref[...] = prolonged(ratio_buf[...] * (coarse_end(0) - sbuf[0]))

    @pl.when(t == 3)
    def _():
        first_near.wait_recv()
        second_near.wait_recv()
        ratio = ratio_buf[...]
        second = ratio * (coarse_end(0) - sbuf[0]) + (coarse_end(1) - sbuf[1])
        out_ref[...] = prolonged(ratio * second)

    @pl.when(t == 1)
    def _():
        out_ref[...] = jnp.zeros_like(out_ref)

    @pl.when(t > 0)
    def _():
        for p in range(S):
            arriving(jsrc.at[p], jbuf.at[p], j_send.at[p], j_recv.at[p], p).wait_recv()
        out_ref[...] += jbuf[...].reshape(NY, NZ)

    for copy in c_copies + k_copies + f_copies:
        copy.wait_send()

    @pl.when(t < T - 1)
    def _():
        for p in range(S):
            jump_copy(p).wait_send()

    @pl.when(t == 0)
    def _():
        for p in range(S):
            coarse_copy(p, 0, 3).wait_send()
            coarse_copy(p, 0, 2).wait_send()

    @pl.when(t == 1)
    def _():
        first_near.wait_send()
        first_far.wait_send()
        for p in range(S):
            coarse_copy(p, 1, 2).wait_send()

    @pl.when(t == 2)
    def _():
        second_near.wait_send()


def fused_body(S, T, state, classes, perm_table, rate_table):
    ny, nz = state.shape[2:]
    rows = ny // S
    slab = rows + 2 * HALO
    field = pltpu.VMEM((S, slab, nz), F32)
    coarse = pltpu.VMEM((ny // 2, nz // 2), F32)
    dma = pltpu.SemaphoreType.DMA
    updated = pl.pallas_call(
        functools.partial(kernel, S, T),
        out_shape=jax.ShapeDtypeStruct((ny, nz), F32),
        in_specs=[pl.BlockSpec(memory_space=pltpu.HBM)] * 4,
        out_specs=pl.BlockSpec(memory_space=pltpu.VMEM),
        scratch_shapes=[
            pltpu.VMEM((ny + 2 * HALO, nz), F32),
            pltpu.VMEM((ny + 2 * HALO, nz), jnp.int32),
            field,
            pltpu.VMEM((S, slab, nz), jnp.int32),
        ] + [field] * 10 + [
            pltpu.SMEM(perm_table.shape, F32),
            pltpu.SMEM(rate_table.shape, F32),
            coarse,
            coarse,
            pltpu.VMEM((FINE, 8, nz // 2), F32),
            pltpu.VMEM((FINE, S, 8, nz // 2), F32),
            pltpu.VMEM((S, rows, nz), F32),
            pltpu.VMEM((S, rows, nz), F32),
            pltpu.VMEM((2, S, rows // 2, nz // 2), F32),
            pltpu.VMEM((S, rows // 2, nz // 2), F32),
            pltpu.VMEM((2, ny // 2, nz // 2), F32),
            pltpu.VMEM((4, ny // 2, nz // 2), F32),
            dma((8,)),
            dma((S - 1,)), dma((S - 1,)),
            dma((S - 1,)), dma((S - 1,)),
            dma((S - 1, T - 1)), dma((S - 1, T - 1)),
            dma((FINE, S - 1)), dma((FINE, S - 1)),
            dma((S,)), dma((S,)),
            dma((2, S)), dma((2, S)),
            dma((2,)), dma((2,)),
        ],
        compiler_params=pltpu.CompilerParams(
            collective_id=0, has_side_effects=True, vmem_limit_bytes=56 * 1024 * 1024),
    )(state[0, 0], classes[0], perm_table, rate_table)
    return updated[None, None]


def with_halo(array, sides, width):
    for axis, dim in sides:
        devices, length = (lax.axis_size(axis), array.shape[dim])
        up = [(i, (i + 1) % devices) for i in range(devices)]
        down = [(j, i) for i, j in up]
        last = lax.slice_in_dim(array, length - width, length, axis=dim)
        first = lax.slice_in_dim(array, 0, width, axis=dim)
        before = lax.ppermute(last, axis, up)
        after = lax.ppermute(first, axis, down)
        array = jnp.concatenate([before, array, after], axis=dim)
    return array


def passed_along(array, axis, by):
    devices = lax.axis_size(axis)
    pairs = [(i, i + by) for i in range(devices) if 0 <= i + by < devices]
    return lax.ppermute(array, axis, pairs)


def lookup(table, classes):
    values = jnp.zeros(classes.shape, jnp.float32)
    for entry in range(table.shape[0]):
        values = jnp.where(classes == entry, table[entry], values)
    return values


def restrict(field):
    cx, ny, nz = field.shape
    return field.reshape(cx, ny // 2, 2, nz // 2, 2).mean(axis=(2, 4))


def prolong(coarse):
    return jnp.repeat(jnp.repeat(coarse, 2, axis=1), 2, axis=2)


def vertical(field):
    zero_plane = jnp.zeros(field.shape[:2] + (1,), jnp.float32)
    upper = jnp.concatenate([field[:, :, 1:], zero_plane], axis=2)
    lower = jnp.concatenate([zero_plane, field[:, :, :-1]], axis=2)
    return (upper, lower)


def operate(field):
    padded = with_halo(field, (("space", 0),), 1)
    upper, lower = vertical(field)
    beside = padded[2:] + padded[:-2]
    beside = beside + jnp.roll(field, -1, 1) + jnp.roll(field, 1, 1)
    beside = beside + upper + lower
    return (1.0 + 6.0 * DIFF) * field - DIFF * beside


def squares(residual):
    return lax.psum(jnp.sum(residual * residual), "space")


def fine_step(field, perm):
    upper, lower = vertical(field)
    rhs = field - ADV * perm * field * (upper - lower)
    solution = field
    residual = rhs - operate(solution)
    direction = residual
    norm_now = squares(residual)
    for step in range(ITERS):
        image = operate(direction)
        alpha = norm_now / lax.psum(jnp.sum(direction * image), "space")
        solution = solution + alpha * direction
        residual = residual - alpha * image
        norm_next = squares(residual)
        direction = residual + norm_next / norm_now * direction
        norm_now = norm_next
    return solution


def body(state, classes, perm_table, rate_table):
    start = state[0]
    perm = lookup(perm_table, classes)
    coarse_ratio = 1.0 / (1.0 + restrict(lookup(rate_table, classes)))
    field = start
    for step in range(FINE):
        field = fine_step(field, perm)
    coarse_start = restrict(start)
    jump = field - prolong(coarse_ratio * coarse_start)
    jump_coarse = restrict(jump)
    first = lax.axis_index("tm") == 0
    factor = jnp.where(first, 0.0, coarse_ratio)
    offset = jnp.where(first, coarse_ratio * coarse_start + jump_coarse, jump_coarse)
    before = passed_along(jump, "tm", 1)
    before_coarse = restrict(before)

    def relay_turn(turn, carry):
        outgoing, received = carry
        received = passed_along(outgoing, "tm", 1)
        return (factor * received + offset, received)

    outgoing, received = lax.fori_loop(
        0, lax.axis_size("tm") - 1, relay_turn, (offset, jnp.zeros_like(offset))
    )
    updated = jnp.where(first, start, before + prolong(received - before_coarse))
    return updated[None]


def solution(mesh):
    placed = (
        P(("groups", "tm"), "space", None, None),
        P(("groups", "space"), None, None),
        P(),
        P(),
    )
    devices, slices = (mesh.shape["space"], mesh.shape["tm"])

    def chosen(state, classes, perm_table, rate_table):
        planes, ny, nz = state.shape[1:]
        fits = planes == 1 and ny // devices >= 4 * HALO and nz == 256
        if fits and slices == 4 and devices >= 3:
            return fused_body(devices, slices, state, classes, perm_table, rate_table)
        return body(state, classes, perm_table, rate_table)

    return jax.shard_map(
        chosen,
        mesh=mesh,
        in_specs=placed,
        out_specs=P(("groups", "tm"), "space", None, None),
        check_vma=False,
    )
```
